32 devices in a mesh: section: 4 (over x, core), seq: 8 (over z, y).
Axes of the slice: x: 2, y: 2, z: 4, core: 2. Of those that a mesh axis runs over, the one named last changes fastest.
Arguments:
- incoming: bfloat16 [4, 8, 16, 24, 320], P(None, 'seq'), may hold values from -6 to 6
- plan: int32 [4], replicated, may hold values from 0 to 3, each once
- waiting: bfloat16 [4, 8, 16, 24, 320], P('section', 'seq'), may hold values from -6 to 6
- spatial_weight: bfloat16 [4, 2, 9, 320, 320], P('section'), may hold values from -0.109375 to 0.109375
- temporal_weight: bfloat16 [4, 2, 3, 320, 320], P('section'), may hold values from -0.1875 to 0.1875
- attn_in: bfloat16 [4, 320, 960], P('section'), may hold values from -5 to 5
- attn_out: bfloat16 [4, 320, 320], P('section'), may hold values from -0.3125 to 0.3125
Outputs:
- outputs: bfloat16 [3, 4, 8, 16, 24, 320], P(None, 'section', 'seq')
The draws below stay inside these ranges and needn't reach their ends.
Inputs may be any that keep to these rules, and one draw needn't show every extreme that they name: `plan`: each of the 4 clip numbers appears once.
All inputs are finite; a program needn't handle non-finite values.
Results may differ from the reference program's by a relative error of at most 0.02.
Values may be sent and summed in bfloat16 or wider, within the bound.
No kernel may reach another device: no remote copies, remote signals or barrier semaphores. Data moves between devices by JAX's collectives and lax.ppermute only.
A program may use at most 64 MiB of HBM per device.

```python
import jax
import jax.numpy as jnp
from jax import lax

C = 320
HEADS = 5
GROUPS = 32
H = 16
W = 24
TICKS = 3
CLIPS = 4
FRAMES = 8
N_SECTION = 4


def draw_attn_in(key, part):
    first_key = jax.random.fold_in(key, 0)
    base = jax.random.normal(first_key, (N_SECTION, C, 3 * C), jnp.float32) * C ** (-0.5)
    return jnp.clip(base, -5.0, 5.0).astype(jnp.bfloat16)


def shard_levels(own_key, extent, cuts, low, high):
    level, own = 1.0, jax.random.fold_in(own_key, 6)
    for dim, blocks in cuts:
        heights = jnp.exp(jax.random.uniform(jax.random.fold_in(own, dim), (blocks,), jnp.float32, low / len(cuts), high / len(cuts)))
        level = level * jnp.repeat(heights, extent[dim] // blocks).reshape([-1 if axis == dim else 1 for axis in range(len(extent))])
    return level


def noise(stream_key, extent, scale, limit, pieces=(), dtype=jnp.bfloat16):
    factor_of = shard_levels(stream_key, extent, pieces, -0.22, 0.18) if pieces else 1.0
    values = jax.random.normal(stream_key, extent, jnp.float32) * scale * factor_of
    return jnp.minimum(jnp.maximum(values, -limit), limit).astype(dtype)


def setup_inputs(seed: int = 0) -> dict:
    splits = jax.random.split(jax.random.key(seed), 8)
    incoming = noise(splits[0], (CLIPS, FRAMES, H, W, C), 1.0, 6.0, ((1, 8),))
    plan = jax.random.permutation(splits[1], CLIPS).astype(jnp.int32)
    waiting = noise(splits[2], (N_SECTION, FRAMES, H, W, C), 1.0, 6.0, ((0, 4), (1, 8)))
    spatial_weight = noise(splits[3], (N_SECTION, 2, 9, C, C), (9 * C) ** -0.5, 0.109375, ((0, 4),))
    temporal_weight = noise(splits[4], (N_SECTION, 2, 3, C, C), (3 * C) ** -0.5, 0.1875, ((0, 4),))
    attn_in = draw_attn_in(jax.random.fold_in(splits[7], 71), 0)
    attn_out = noise(splits[6], (N_SECTION, C, C), C ** -0.5, 0.3125, ((0, 4),))
    return dict(incoming=incoming, plan=plan, waiting=waiting, spatial_weight=spatial_weight, temporal_weight=temporal_weight, attn_in=attn_in, attn_out=attn_out)


EPSILON = 1e-05

def group_norm(values):
    frames, height, width, channels = values.shape
    grouped = values.astype(jnp.float32).reshape(frames, height * width, GROUPS, channels // GROUPS)
    center = lax.optimization_barrier(jnp.mean(grouped, axis=(1, 3), keepdims=True))
    spread = lax.optimization_barrier(jnp.mean(jnp.square(grouped - center), axis=(1, 3), keepdims=True))
    normed = (grouped - center) * lax.rsqrt(spread + EPSILON)
    return normed.reshape(frames, height, width, channels)

def layer_norm(values):
    floats = values.astype(jnp.float32)
    center = lax.optimization_barrier(jnp.mean(floats, axis=-1, keepdims=True))
    spread = lax.optimization_barrier(jnp.mean(jnp.square(floats - center), axis=-1, keepdims=True))
    return (floats - center) * lax.rsqrt(spread + EPSILON)

def spatial_conv(values, kernel):
    frames, height, width, channels = values.shape
    padded = jnp.pad(values, ((0, 0), (1, 1), (1, 1), (0, 0)))
    total = jnp.zeros((frames * height * width, kernel.shape[2]), jnp.float32)
    for offset in range(9):
        row_shift = offset // 3
        col_shift = offset % 3
        window = padded[:, row_shift:row_shift + height, col_shift:col_shift + width, :].reshape(-1, channels)
        total = total + jnp.dot(window, kernel[offset], preferred_element_type=jnp.float32)
    return total.reshape(frames, height, width, -1)

def temporal_conv(values, kernel):
    frames, items, channels = values.shape
    padded = jnp.pad(values, ((1, 1), (0, 0), (0, 0)))
    total = jnp.zeros((frames * items, kernel.shape[2]), jnp.float32)
    for offset in range(3):
        window = padded[offset:offset + frames].reshape(-1, channels)
        total = total + jnp.dot(window, kernel[offset], preferred_element_type=jnp.float32)
    return total.reshape(frames, items, -1)

def spatial_part(values, kernels):
    first_in = jax.nn.silu(group_norm(values)).astype(jnp.bfloat16)
    middle = spatial_conv(first_in, kernels[0]).astype(jnp.bfloat16)
    second_in = jax.nn.silu(group_norm(middle)).astype(jnp.bfloat16)
    return (values.astype(jnp.float32) + spatial_conv(second_in, kernels[1])).astype(jnp.bfloat16)

def temporal_convs(values, kernels):
    first_in = jax.nn.silu(layer_norm(values)).astype(jnp.bfloat16)
    middle = temporal_conv(first_in, kernels[0]).astype(jnp.bfloat16)
    second_in = jax.nn.silu(layer_norm(middle)).astype(jnp.bfloat16)
    return (values.astype(jnp.float32) + temporal_conv(second_in, kernels[1])).astype(jnp.bfloat16)

def attention(values, packed, outward):
    frames, items, channels = values.shape
    head_size = channels // HEADS
    normed = layer_norm(values).astype(jnp.bfloat16)
    projected = jnp.dot(normed.reshape(-1, channels), packed, preferred_element_type=jnp.float32).astype(jnp.bfloat16)
    projected = projected.reshape(frames, items, 3, HEADS, head_size)
    queries = projected[:, :, 0].astype(jnp.float32)
    keys_all = projected[:, :, 1].astype(jnp.float32)
    values_all = projected[:, :, 2].astype(jnp.float32)
    scores = jnp.einsum('fkhd,gkhd->khfg', queries, keys_all) * head_size ** (-0.5)
    weights = jax.nn.softmax(scores, axis=-1).astype(jnp.bfloat16)
    mixed = jnp.einsum('khfg,gkhd->fkhd', weights.astype(jnp.float32), values_all).astype(jnp.bfloat16)
    result = values.astype(jnp.float32).reshape(-1, channels) + jnp.dot(mixed.reshape(-1, channels), outward, preferred_element_type=jnp.float32)
    return result.reshape(frames, items, channels).astype(jnp.bfloat16)

def section_block(clip, spatial_kernels, temporal_kernels, packed, outward):
    frames, height, width, channels = clip.shape
    after_spatial = spatial_part(clip, spatial_kernels)
    flat = after_spatial.reshape(frames, height * width, channels)
    after_convs = temporal_convs(flat, temporal_kernels)
    finished = attention(after_convs, packed, outward)
    return finished.reshape(frames, height, width, channels)

def reference(incoming, plan, waiting, spatial_weight, temporal_weight, attn_in, attn_out):
    current = [waiting[section_number] for section_number in range(N_SECTION)]
    collected = []
    previous = current
    for tick_index in range(TICKS):
        if tick_index > 0:
            entering = lax.dynamic_index_in_dim(incoming, plan[tick_index - 1], 0, keepdims=False)
            current = [entering] + previous[:-1]
        previous = [section_block(current[section_number], spatial_weight[section_number], temporal_weight[section_number], attn_in[section_number], attn_out[section_number]) for section_number in range(N_SECTION)]
        collected.append(jnp.stack(previous))
    return jnp.stack(collected)
```

```python
import functools

import jax
import jax.numpy as jnp
from jax import lax
from jax.experimental import pallas as pl
from jax.experimental.pallas import tpu as pltpu
from jax.sharding import PartitionSpec as P

HEADS = 5
GROUPS = 32
TICKS = 3
EPSILON = 1e-05
MIB = 1 << 20


def silu(values):
    half = 0.5 * values
    return half + half * jnp.tanh(half)


def bucket(shape, dim, size):
    index = lax.broadcasted_iota(jnp.int32, shape, dim).astype(jnp.float32)
    return jnp.floor((index + 0.5) * (1.0 / size))


def within(shape, dim, size):
    index = lax.broadcasted_iota(jnp.int32, shape, dim).astype(jnp.float32)
    return index - size * jnp.floor((index + 0.5) * (1.0 / size))


def group_total(partial, same_group):
    high = partial.astype(jnp.bfloat16).astype(jnp.float32)
    rest = partial - high
    middle = rest.astype(jnp.bfloat16).astype(jnp.float32)
    low = rest - middle
    rows = jnp.concatenate([high, middle, low, jnp.zeros_like(low)], axis=0).astype(jnp.bfloat16)
    sums = jnp.dot(rows, same_group, preferred_element_type=jnp.float32)
    return jnp.sum(sums, axis=0, keepdims=True)


def group_norm(values, same_group):
    cells, channels = values.shape
    scale = 1.0 / (cells * (channels // GROUPS))
    center = group_total(jnp.sum(values.reshape(-1, 8, channels), axis=0), same_group) * scale
    shifted = values - center
    spread = group_total(jnp.sum(jnp.square(shifted).reshape(-1, 8, channels), axis=0), same_group) * scale
    return shifted * lax.rsqrt(spread + EPSILON)


def layer_norm(values):
    center = jnp.mean(values, axis=-1, keepdims=True)
    shifted = values - center
    spread = jnp.mean(jnp.square(shifted), axis=-1, keepdims=True)
    return shifted * lax.rsqrt(spread + EPSILON)


def spatial_kernel(height, width, picks, *refs):
    if picks:
        pick_ref, entering_ref, passed_ref, weight_ref, out_ref, kernels, taps, sems = refs
    else:
        passed_ref, weight_ref, out_ref, kernels, taps, sems = refs
    cells, channels = out_ref.shape
    copies = []
    for layer in range(2):
        for row in range(3):
            copy = pltpu.make_async_copy(
                weight_ref.at[layer, row], kernels.at[layer, row], sems.at[layer, row]
            )
            copy.start()
            copies.append(copy)
    edge = jnp.zeros((width, 3 * channels), jnp.bfloat16)
    taps[0:width, :] = edge
    taps[width + cells : 2 * width + cells, :] = edge
    same_group = (
        bucket((channels, channels), 0, channels // GROUPS)
        == bucket((channels, channels), 1, channels // GROUPS)
    ).astype(jnp.float32).astype(jnp.bfloat16)
    column = lax.broadcasted_iota(jnp.int32, (1, width, channels), 1)

    def conv(values, layer):
        framed = values.reshape(height, width, channels)
        left = jnp.where(column == 0, 0.0, pltpu.roll(framed, 1, 1)).reshape(cells, channels)
        right = jnp.where(column == width - 1, 0.0, pltpu.roll(framed, width - 1, 1)).reshape(cells, channels)
        taps[width : width + cells, 0:channels] = left.astype(jnp.bfloat16)
        taps[width : width + cells, channels : 2 * channels] = values.astype(jnp.bfloat16)
        taps[width : width + cells, 2 * channels : 3 * channels] = right.astype(jnp.bfloat16)
        total = None
        for row in range(3):
            copies[3 * layer + row].wait()
            part = jnp.dot(
                taps[row * width : row * width + cells, :],
                kernels[layer, row],
                preferred_element_type=jnp.float32,
            )
            total = part if total is None else total + part
        return total

    start = passed_ref[...]
    if picks:
        start = jnp.where(pick_ref[0] == 1, entering_ref[...], start)
    start = start.astype(jnp.float32)
    middle = conv(silu(group_norm(start, same_group)), 0).astype(jnp.bfloat16).astype(jnp.float32)
    after = conv(silu(group_norm(middle, same_group)), 1)
    out_ref[...] = (start + after).astype(jnp.bfloat16)


def spatial_part(height, width, passed, weights, picked=None, entering=None):
    cells, channels = passed.shape
    weights = weights.reshape(2, 3, 3 * channels, weights.shape[-1])
    specs = [
        pl.BlockSpec((cells, channels), lambda i, *_: (0, 0)),
        pl.BlockSpec(memory_space=pl.ANY),
    ]
    operands = [passed, weights]
    if picked is not None:
        specs = [pl.BlockSpec((None, cells, channels), lambda i, pick: (pick[1], 0, 0))] + specs
        operands = [picked, entering] + operands
    return pl.pallas_call(
        functools.partial(spatial_kernel, height, width, picked is not None),
        out_shape=jax.ShapeDtypeStruct((cells, channels), jnp.bfloat16),
        grid_spec=pltpu.PrefetchScalarGridSpec(
            num_scalar_prefetch=0 if picked is None else 1,
            grid=(1,),
            in_specs=specs,
            out_specs=pl.BlockSpec((cells, channels), lambda i, *_: (0, 0)),
            scratch_shapes=[
                pltpu.VMEM(weights.shape, jnp.bfloat16),
                pltpu.VMEM((cells + 2 * width, 3 * channels), jnp.bfloat16),
                pltpu.SemaphoreType.DMA((2, 3)),
            ],
        ),
        compiler_params=pltpu.CompilerParams(vmem_limit_bytes=24 * MIB),
    )(*operands)


def temporal_kernel(frames, items, in_ref, conv_ref, packed_ref, outward_ref, out_ref, kernels, packed, outward, taps, sems):
    rows, channels = out_ref.shape
    copies = [
        pltpu.make_async_copy(conv_ref.at[0], kernels.at[0], sems.at[0]),
        pltpu.make_async_copy(conv_ref.at[1], kernels.at[1], sems.at[1]),
        pltpu.make_async_copy(packed_ref, packed, sems.at[2]),
        pltpu.make_async_copy(outward_ref, outward, sems.at[3]),
    ]
    for copy in copies:
        copy.start()
    aligned = items % 16 == 0

    def conv(values, layer):
        if aligned:
            whole = values.astype(jnp.bfloat16)
            edge = jnp.zeros((items, channels), jnp.bfloat16)
            taps[0:items, 0:channels] = edge
            taps[items:rows, 0:channels] = whole[0 : rows - items]
            taps[:, channels : 2 * channels] = whole
            taps[0 : rows - items, 2 * channels : 3 * channels] = whole[items:rows]
            taps[rows - items : rows, 2 * channels : 3 * channels] = edge
        else:
            row = lax.broadcasted_iota(jnp.int32, (rows, channels), 0)
            before = jnp.where(row < items, 0.0, pltpu.roll(values, items, 0))
            behind = jnp.where(row >= rows - items, 0.0, pltpu.roll(values, rows - items, 0))
            taps[:, 0:channels] = before.astype(jnp.bfloat16)
            taps[:, channels : 2 * channels] = values.astype(jnp.bfloat16)
            taps[:, 2 * channels : 3 * channels] = behind.astype(jnp.bfloat16)
        copies[layer].wait()
        return jnp.dot(taps[...], kernels[layer], preferred_element_type=jnp.float32)

    start = in_ref[...].astype(jnp.float32)
    middle = conv(silu(layer_norm(start)), 0).astype(jnp.bfloat16).astype(jnp.float32)
    after = (start + conv(silu(layer_norm(middle)), 1)).astype(jnp.bfloat16).astype(jnp.float32)

    normed = layer_norm(after).astype(jnp.bfloat16)
    copies[2].wait()
    taps[...] = jnp.dot(normed, packed[...], preferred_element_type=jnp.float32).astype(jnp.bfloat16)
    queries = taps[:, 0:channels]
    keys = taps[:, channels : 2 * channels]
    values = taps[:, 2 * channels : 3 * channels]

    head_size = channels // HEADS
    block = 16 if aligned else items
    size = frames * block
    apart = within((size, size), 0, block) != within((size, size), 1, block)
    blocked = jnp.where(apart, -1e30, 0.0)
    copies[3].wait()
    mixed_blocks = []
    for first in range(0, items, block):
        def part(whole):
            if block == items:
                return whole
            return jnp.concatenate(
                [whole[f * items + first : f * items + first + block] for f in range(frames)], axis=0
            )

        q, k, v = part(queries), part(keys), part(values)
        mixed = []
        for head in range(HEADS):
            lanes = slice(head * head_size, (head + 1) * head_size)
            scores = lax.dot_general(
                q[:, lanes], k[:, lanes], (((1,), (1,)), ((), ())), preferred_element_type=jnp.float32
            ) * head_size ** (-0.5) + blocked
            top = jnp.max(scores, axis=-1, keepdims=True)
            raised = jnp.exp(scores - top)
            weights = (raised / jnp.sum(raised, axis=-1, keepdims=True)).astype(jnp.bfloat16)
            mixed.append(jnp.dot(weights, v[:, lanes], preferred_element_type=jnp.float32))
        mixed_blocks.append(jnp.concatenate(mixed, axis=1).astype(jnp.bfloat16))
    if len(mixed_blocks) == 1:
        mixed = mixed_blocks[0]
    else:
        mixed = jnp.concatenate(
            [piece[f * block : (f + 1) * block] for f in range(frames) for piece in mixed_blocks], axis=0
        )
    result = after + jnp.dot(mixed, outward[...], preferred_element_type=jnp.float32)
    out_ref[...] = result.astype(jnp.bfloat16)


def temporal_part(frames, items, values, kernels, packed, outward):
    rows, channels = values.shape
    kernels = kernels.reshape(2, 3 * channels, kernels.shape[-1])
    anywhere = pl.BlockSpec(memory_space=pl.ANY)
    return pl.pallas_call(
        functools.partial(temporal_kernel, frames, items),
        out_shape=jax.ShapeDtypeStruct((rows, channels), jnp.bfloat16),
        in_specs=[pl.BlockSpec(memory_space=pltpu.VMEM), anywhere, anywhere, anywhere],
        out_specs=pl.BlockSpec(memory_space=pltpu.VMEM),
        scratch_shapes=[
            pltpu.VMEM(kernels.shape, jnp.bfloat16),
            pltpu.VMEM(packed.shape, jnp.bfloat16),
            pltpu.VMEM(outward.shape, jnp.bfloat16),
            pltpu.VMEM((rows, 3 * channels), jnp.bfloat16),
            pltpu.SemaphoreType.DMA((4,)),
        ],
        compiler_params=pltpu.CompilerParams(vmem_limit_bytes=24 * MIB),
    )(values, kernels, packed, outward)


def shards(incoming, plan, waiting, spatial_weight, temporal_weight, attn_in, attn_out):
    clips, _, height, width, channels = incoming.shape
    cells = height * width
    devices = lax.axis_size("seq")
    share = cells // devices
    sections = lax.axis_size("section")
    first_section = (lax.axis_index("section") == 0).astype(jnp.int32)
    entering = incoming.reshape(clips, cells, channels)
    current = waiting.reshape(cells, channels)
    collected = []
    for tick in range(TICKS):
        if tick == 0:
            after = spatial_part(height, width, current, spatial_weight[0])
        else:
            ring = [(i, (i + 1) % sections) for i in range(sections)]
            passed = lax.ppermute(current, "section", ring)
            picked = jnp.stack([first_section, plan[tick - 1]])
            after = spatial_part(height, width, passed, spatial_weight[0], picked, entering)
        grouped = after.reshape(devices, share, channels)
        gathered = lax.all_to_all(grouped, "seq", split_axis=0, concat_axis=0, tiled=True)
        done = temporal_part(
            devices, share, gathered.reshape(devices * share, channels), temporal_weight[0], attn_in[0], attn_out[0]
        )
        back = lax.all_to_all(
            done.reshape(devices, share, channels), "seq", split_axis=0, concat_axis=0, tiled=True
        )
        current = back.reshape(cells, channels)
        collected.append(current.reshape(height, width, channels))
    return jnp.stack(collected)[:, None, None]


def solution(mesh):
    return jax.shard_map(
        shards,
        mesh=mesh,
        in_specs=(
            P(None, "seq", None, None, None),
            P(),
            P("section", "seq", None, None, None),
            P("section", None, None, None, None),
            P("section", None, None, None, None),
            P("section", None, None),
            P("section", None, None),
        ),
        out_specs=P(None, "section", "seq", None, None, None),
        check_vma=False,
    )
```

```python
import functools

import jax
import jax.numpy as jnp
from jax import lax
from jax.experimental import pallas as pl
from jax.experimental.pallas import tpu as pltpu
from jax.sharding import PartitionSpec as P

HEADS = 5
GROUPS = 32
TICKS = 3
EPSILON = 1e-05
MIB = 1 << 20


def silu(values):
    half = 0.5 * values
    return half + half * jnp.tanh(half)


def bucket(shape, dim, size):
    index = lax.broadcasted_iota(jnp.int32, shape, dim).astype(jnp.float32)
    return jnp.floor((index + 0.5) * (1.0 / size))


def within(shape, dim, size):
    index = lax.broadcasted_iota(jnp.int32, shape, dim).astype(jnp.float32)
    return index - size * jnp.floor((index + 0.5) * (1.0 / size))


def group_total(partial, same_group):
    high = partial.astype(jnp.bfloat16).astype(jnp.float32)
    rest = partial - high
    middle = rest.astype(jnp.bfloat16).astype(jnp.float32)
    low = rest - middle
    rows = jnp.concatenate([high, middle, low, jnp.zeros_like(low)], axis=0).astype(jnp.bfloat16)
    sums = jnp.dot(rows, same_group, preferred_element_type=jnp.float32)
    return jnp.sum(sums, axis=0, keepdims=True)


def group_norm(values, same_group):
    cells, channels = values.shape
    scale = 1.0 / (cells * (channels // GROUPS))
    center = group_total(jnp.sum(values.reshape(-1, 8, channels), axis=0), same_group) * scale
    shifted = values - center
    spread = group_total(jnp.sum(jnp.square(shifted).reshape(-1, 8, channels), axis=0), same_group) * scale
    return shifted * lax.rsqrt(spread + EPSILON)


def layer_norm(values):
    center = jnp.mean(values, axis=-1, keepdims=True)
    shifted = values - center
    spread = jnp.mean(jnp.square(shifted), axis=-1, keepdims=True)
    return shifted * lax.rsqrt(spread + EPSILON)


def spatial_kernel(height, width, picks, *refs):
    if picks:
        _, entering_ref, passed_ref, weight_ref, out_ref, kernels, taps, sems = refs
    else:
        passed_ref, weight_ref, out_ref, kernels, taps, sems = refs
    cells, channels = out_ref.shape
    copies = []
    for layer in range(2):
        for row in range(3):
            copy = pltpu.make_async_copy(
                weight_ref.at[layer, row], kernels.at[layer, row], sems.at[layer, row]
            )
            copy.start()
            copies.append(copy)
    edge = jnp.zeros((width, 3 * channels), jnp.bfloat16)
    taps[0:width, :] = edge
    taps[width + cells : 2 * width + cells, :] = edge
    same_group = (
        bucket((channels, channels), 0, channels // GROUPS)
        == bucket((channels, channels), 1, channels // GROUPS)
    ).astype(jnp.float32).astype(jnp.bfloat16)
    column = lax.broadcasted_iota(jnp.int32, (1, width, channels), 1)

    def conv(values, layer):
        framed = values.reshape(height, width, channels)
        left = jnp.where(column == 0, 0.0, pltpu.roll(framed, 1, 1)).reshape(cells, channels)
        right = jnp.where(column == width - 1, 0.0, pltpu.roll(framed, width - 1, 1)).reshape(cells, channels)
        taps[width : width + cells, 0:channels] = left.astype(jnp.bfloat16)
        taps[width : width + cells, channels : 2 * channels] = values.astype(jnp.bfloat16)
        taps[width : width + cells, 2 * channels : 3 * channels] = right.astype(jnp.bfloat16)
        total = None
        for row in range(3):
            copies[3 * layer + row].wait()
            part = jnp.dot(
                taps[row * width : row * width + cells, :],
                kernels[layer, row],
                preferred_element_type=jnp.float32,
            )
            total = part if total is None else total + part
        return total

    start = passed_ref[...]
    if picks:
        start = jnp.where(lax.axis_index("section") == 0, entering_ref[...], start)
    start = start.astype(jnp.float32)
    middle = conv(silu(group_norm(start, same_group)), 0).astype(jnp.bfloat16).astype(jnp.float32)
    after = conv(silu(group_norm(middle, same_group)), 1)
    out_ref[...] = (start + after).astype(jnp.bfloat16)


def spatial_part(height, width, passed, weights, plan=None, entering=None, turn=0):
    cells, channels = passed.shape
    weights = weights.reshape(2, 3, 3 * channels, weights.shape[-1])
    specs = [
        pl.BlockSpec((cells, channels), lambda i, *_: (0, 0)),
        pl.BlockSpec(memory_space=pltpu.HBM),
    ]
    operands = [passed, weights]
    if plan is not None:
        specs = [pl.BlockSpec((None, cells, channels), lambda i, order: (order[turn], 0, 0))] + specs
        operands = [plan, entering] + operands
    return pl.pallas_call(
        functools.partial(spatial_kernel, height, width, plan is not None),
        out_shape=jax.ShapeDtypeStruct((cells, channels), jnp.bfloat16),
        grid_spec=pltpu.PrefetchScalarGridSpec(
            num_scalar_prefetch=0 if plan is None else 1,
            grid=(1,),
            in_specs=specs,
            out_specs=pl.BlockSpec((cells, channels), lambda i, *_: (0, 0)),
            scratch_shapes=[
                pltpu.VMEM(weights.shape, jnp.bfloat16),
                pltpu.VMEM((cells + 2 * width, 3 * channels), jnp.bfloat16),
                pltpu.SemaphoreType.DMA((2, 3)),
            ],
        ),
        compiler_params=pltpu.CompilerParams(vmem_limit_bytes=24 * MIB),
    )(*operands)


def temporal_kernel(frames, items, in_ref, conv_ref, packed_ref, outward_ref, out_ref, kernels, packed, outward, taps, sems):
    rows, channels = out_ref.shape
    copies = [
        pltpu.make_async_copy(conv_ref.at[0], kernels.at[0], sems.at[0]),
        pltpu.make_async_copy(conv_ref.at[1], kernels.at[1], sems.at[1]),
        pltpu.make_async_copy(packed_ref, packed, sems.at[2]),
        pltpu.make_async_copy(outward_ref, outward, sems.at[3]),
    ]
    for copy in copies:
        copy.start()
    aligned = items % 16 == 0

    def conv(values, layer):
        if aligned:
            whole = values.astype(jnp.bfloat16)
            edge = jnp.zeros((items, channels), jnp.bfloat16)
            taps[0:items, 0:channels] = edge
            taps[items:rows, 0:channels] = whole[0 : rows - items]
            taps[:, channels : 2 * channels] = whole
            taps[0 : rows - items, 2 * channels : 3 * channels] = whole[items:rows]
            taps[rows - items : rows, 2 * channels : 3 * channels] = edge
        else:
            row = lax.broadcasted_iota(jnp.int32, (rows, channels), 0)
            before = jnp.where(row < items, 0.0, pltpu.roll(values, items, 0))
            behind = jnp.where(row >= rows - items, 0.0, pltpu.roll(values, rows - items, 0))
            taps[:, 0:channels] = before.astype(jnp.bfloat16)
            taps[:, channels : 2 * channels] = values.astype(jnp.bfloat16)
            taps[:, 2 * channels : 3 * channels] = behind.astype(jnp.bfloat16)
        copies[layer].wait()
        return jnp.dot(taps[...], kernels[layer], preferred_element_type=jnp.float32)

    start = in_ref[...].astype(jnp.float32)
    middle = conv(silu(layer_norm(start)), 0).astype(jnp.bfloat16).astype(jnp.float32)
    after = (start + conv(silu(layer_norm(middle)), 1)).astype(jnp.bfloat16).astype(jnp.float32)

    normed = layer_norm(after).astype(jnp.bfloat16)
    copies[2].wait()
    taps[...] = jnp.dot(normed, packed[...], preferred_element_type=jnp.float32).astype(jnp.bfloat16)
    queries = taps[:, 0:channels]
    keys = taps[:, channels : 2 * channels]
    values = taps[:, 2 * channels : 3 * channels]

    head_size = channels // HEADS
    block = 16 if aligned else items
    size = frames * block
    apart = within((size, size), 0, block) != within((size, size), 1, block)
    blocked = jnp.where(apart, -1e30, 0.0)
    copies[3].wait()
    mixed_blocks = []
    for first in range(0, items, block):
        def part(whole):
            if block == items:
                return whole
            return jnp.concatenate(
                [whole[f * items + first : f * items + first + block] for f in range(frames)], axis=0
            )

        q, k, v = part(queries), part(keys), part(values)
        mixed = []
        for head in range(HEADS):
            lanes = slice(head * head_size, (head + 1) * head_size)
            scores = lax.dot_general(
                q[:, lanes], k[:, lanes], (((1,), (1,)), ((), ())), preferred_element_type=jnp.float32
            ) * head_size ** (-0.5) + blocked
            top = jnp.max(scores, axis=-1, keepdims=True)
            raised = jnp.exp(scores - top)
            weights = (raised / jnp.sum(raised, axis=-1, keepdims=True)).astype(jnp.bfloat16)
            mixed.append(jnp.dot(weights, v[:, lanes], preferred_element_type=jnp.float32))
        mixed_blocks.append(jnp.concatenate(mixed, axis=1).astype(jnp.bfloat16))
    if len(mixed_blocks) == 1:
        mixed = mixed_blocks[0]
    else:
        mixed = jnp.concatenate(
            [piece[f * block : (f + 1) * block] for f in range(frames) for piece in mixed_blocks], axis=0
        )
    result = after + jnp.dot(mixed, outward[...], preferred_element_type=jnp.float32)
    out_ref[...] = result.astype(jnp.bfloat16)


def temporal_part(frames, items, values, kernels, packed, outward):
    rows, channels = values.shape
    kernels = kernels.reshape(2, 3 * channels, kernels.shape[-1])
    anywhere = pl.BlockSpec(memory_space=pltpu.HBM)
    return pl.pallas_call(
        functools.partial(temporal_kernel, frames, items),
        out_shape=jax.ShapeDtypeStruct((rows, channels), jnp.bfloat16),
        in_specs=[pl.BlockSpec(memory_space=pltpu.VMEM), anywhere, anywhere, anywhere],
        out_specs=pl.BlockSpec(memory_space=pltpu.VMEM),
        scratch_shapes=[
            pltpu.VMEM(kernels.shape, jnp.bfloat16),
            pltpu.VMEM(packed.shape, jnp.bfloat16),
            pltpu.VMEM(outward.shape, jnp.bfloat16),
            pltpu.VMEM((rows, 3 * channels), jnp.bfloat16),
            pltpu.SemaphoreType.DMA((4,)),
        ],
        compiler_params=pltpu.CompilerParams(vmem_limit_bytes=24 * MIB),
    )(values, kernels, packed, outward)


def assemble_kernel(*refs):
    *parts, out_ref, sems = refs
    copies = [pltpu.make_async_copy(part, out_ref.at[i], sems.at[i]) for i, part in enumerate(parts)]
    for copy in copies:
        copy.start()
    for copy in copies:
        copy.wait()


def assembled(parts):
    return pl.pallas_call(
        assemble_kernel,
        out_shape=jax.ShapeDtypeStruct((len(parts),) + parts[0].shape, parts[0].dtype),
        in_specs=[pl.BlockSpec(memory_space=pl.ANY)] * len(parts),
        out_specs=pl.BlockSpec(memory_space=pl.ANY),
        scratch_shapes=[pltpu.SemaphoreType.DMA((len(parts),))],
        compiler_params=pltpu.CompilerParams(vmem_limit_bytes=MIB),
    )(*parts)


def shards(incoming, plan, waiting, spatial_weight, temporal_weight, attn_in, attn_out):
    clips, _, height, width, channels = incoming.shape
    cells = height * width
    devices = lax.axis_size("seq")
    share = cells // devices
    sections = lax.axis_size("section")
    entering = incoming.reshape(clips, cells, channels)
    current = waiting.reshape(cells, channels)
    collected = []
    for tick in range(TICKS):
        if tick == 0:
            after = spatial_part(height, width, current, spatial_weight[0])
        else:
            ring = [(i, (i + 1) % sections) for i in range(sections)]
            passed = lax.ppermute(current, "section", ring)
            after = spatial_part(height, width, passed, spatial_weight[0], plan, entering, tick - 1)
        grouped = after.reshape(devices, share, channels)
        gathered = lax.all_to_all(grouped, "seq", split_axis=0, concat_axis=0, tiled=True)
        done = temporal_part(
            devices, share, gathered.reshape(devices * share, channels), temporal_weight[0], attn_in[0], attn_out[0]
        )
        back = lax.all_to_all(
            done.reshape(devices, share, channels), "seq", split_axis=0, concat_axis=0, tiled=True
        )
        current = back.reshape(cells, channels)
        collected.append(current)
    return assembled(collected).reshape(TICKS, 1, 1, height, width, channels)


def solution(mesh):
    return jax.shard_map(
        shards,
        mesh=mesh,
        in_specs=(
            P(None, "seq", None, None, None),
            P(),
            P("section", "seq", None, None, None),
            P("section", None, None, None, None),
            P("section", None, None, None, None),
            P("section", None, None),
            P("section", None, None),
        ),
        out_specs=P(None, "section", "seq", None, None, None),
        check_vma=False,
    )
```

```python
import functools

import jax
import jax.numpy as jnp
from jax import lax
from jax.experimental import pallas as pl
from jax.experimental.pallas import tpu as pltpu
from jax.sharding import PartitionSpec as P

HEADS = 5
GROUPS = 32
TICKS = 3
EPSILON = 1e-05
MIB = 1 << 20
LANES = 128
LOG2_E = 1.4426950408889634


def silu(values):
    half = 0.5 * values
    return half + half * jnp.tanh(half)


def bucket(shape, dim, size):
    index = lax.broadcasted_iota(jnp.int32, shape, dim).astype(jnp.float32)
    return jnp.floor((index + 0.5) * (1.0 / size))


def within(shape, dim, size):
    index = lax.broadcasted_iota(jnp.int32, shape, dim).astype(jnp.float32)
    return index - size * jnp.floor((index + 0.5) * (1.0 / size))


def group_total(partial, same_group):
    high = partial.astype(jnp.bfloat16).astype(jnp.float32)
    rest = partial - high
    middle = rest.astype(jnp.bfloat16).astype(jnp.float32)
    low = rest - middle
    rows = jnp.concatenate([high, middle, low, jnp.zeros_like(low)], axis=0).astype(jnp.bfloat16)
    sums = jnp.dot(rows, same_group, preferred_element_type=jnp.float32)
    return jnp.sum(sums, axis=0, keepdims=True)


def group_norm(values, same_group):
    cells, channels = values.shape
    scale = 1.0 / (cells * (channels // GROUPS))
    center = group_total(jnp.sum(values.reshape(-1, 8, channels), axis=0), same_group) * scale
    shifted = values - center
    spread = group_total(jnp.sum(jnp.square(shifted).reshape(-1, 8, channels), axis=0), same_group) * scale
    return shifted * lax.rsqrt(spread + EPSILON)


def layer_norm(values, ones):
    channels = values.shape[-1]

    def across(sums):
        pieces = -(-channels // sums.shape[-1])
        return jnp.concatenate([sums] * pieces, axis=-1)[:, :channels]

    floats = values.astype(jnp.float32)
    center = jnp.dot(values, ones, preferred_element_type=jnp.float32) * (1.0 / channels)
    shifted = floats - across(center)
    squares = jnp.square(shifted).astype(jnp.bfloat16)
    spread = jnp.dot(squares, ones, preferred_element_type=jnp.float32) * (1.0 / channels)
    return shifted * across(lax.rsqrt(spread + EPSILON))


def spatial_kernel(height, width, picks, stream, *refs):
    if picks:
        _, entering_ref, *refs = refs
    passed_ref, weight_ref, out_ref, taps, *refs = refs
    cells, channels = out_ref.shape
    copies = []
    kernels = weight_ref
    if stream:
        kernels, sems = refs
        for layer in range(2):
            for row in range(3):
                copy = pltpu.make_async_copy(
                    weight_ref.at[layer, row], kernels.at[layer, row], sems.at[layer, row]
                )
                copy.start()
                copies.append(copy)
    edge = jnp.zeros((width, 3 * channels), jnp.bfloat16)
    taps[0:width, :] = edge
    taps[width + cells : 2 * width + cells, :] = edge
    same_group = (
        bucket((channels, channels), 0, channels // GROUPS)
        == bucket((channels, channels), 1, channels // GROUPS)
    ).astype(jnp.float32).astype(jnp.bfloat16)
    column = lax.broadcasted_iota(jnp.int32, (1, width, channels), 1)

    def conv(values, layer):
        framed = values.reshape(height, width, channels)
        left = jnp.where(column == 0, 0.0, pltpu.roll(framed, 1, 1)).reshape(cells, channels)
        right = jnp.where(column == width - 1, 0.0, pltpu.roll(framed, width - 1, 1)).reshape(cells, channels)
        taps[width : width + cells, 0:channels] = left.astype(jnp.bfloat16)
        taps[width : width + cells, channels : 2 * channels] = values.astype(jnp.bfloat16)
        taps[width : width + cells, 2 * channels : 3 * channels] = right.astype(jnp.bfloat16)
        total = None
        for row in range(3):
            if stream:
                copies[3 * layer + row].wait()
            part = jnp.dot(
                taps[row * width : row * width + cells, :],
                kernels[layer, row],
                preferred_element_type=jnp.float32,
            )
            total = part if total is None else total + part
        return total

    start = passed_ref[...]
    if picks:
        start = jnp.where(lax.axis_index("section") == 0, entering_ref[...], start)
    start = start.astype(jnp.float32)
    middle = conv(silu(group_norm(start, same_group)), 0).astype(jnp.bfloat16).astype(jnp.float32)
    after = conv(silu(group_norm(middle, same_group)), 1)
    out_ref[...] = (start + after).astype(jnp.bfloat16)


def spatial_part(height, width, passed, weights, plan=None, entering=None, turn=0):
    cells, channels = passed.shape
    weights = weights.reshape(2, 3, 3 * channels, weights.shape[-1])
    stream = plan is None
    specs = [
        pl.BlockSpec((cells, channels), lambda i, *_: (0, 0)),
        pl.BlockSpec(memory_space=pltpu.HBM if stream else pltpu.VMEM),
    ]
    operands = [passed, weights]
    if plan is not None:
        specs = [pl.BlockSpec((None, cells, channels), lambda i, order: (order[turn], 0, 0))] + specs
        operands = [plan, entering] + operands
    return pl.pallas_call(
        functools.partial(spatial_kernel, height, width, plan is not None, stream),
        out_shape=jax.ShapeDtypeStruct((cells, channels), jnp.bfloat16),
        grid_spec=pltpu.PrefetchScalarGridSpec(
            num_scalar_prefetch=0 if plan is None else 1,
            grid=(1,),
            in_specs=specs,
            out_specs=pl.BlockSpec((cells, channels), lambda i, *_: (0, 0)),
            scratch_shapes=[pltpu.VMEM((cells + 2 * width, 3 * channels), jnp.bfloat16)]
            + ([pltpu.VMEM(weights.shape, jnp.bfloat16), pltpu.SemaphoreType.DMA((2, 3))] if stream else []),
        ),
        compiler_params=pltpu.CompilerParams(vmem_limit_bytes=(58 if stream else 24) * MIB),
    )(*operands)


def temporal_kernel(frames, items, in_ref, kernels, packed, outward, out_ref, taps):
    rows, channels = out_ref.shape
    aligned = items % 16 == 0

    def conv(values, layer):
        if aligned:
            whole = values.astype(jnp.bfloat16)
            edge = jnp.zeros((items, channels), jnp.bfloat16)
            taps[0:items, 0:channels] = edge
            taps[items:rows, 0:channels] = whole[0 : rows - items]
            taps[:, channels : 2 * channels] = whole
            taps[0 : rows - items, 2 * channels : 3 * channels] = whole[items:rows]
            taps[rows - items : rows, 2 * channels : 3 * channels] = edge
        else:
            row = lax.broadcasted_iota(jnp.int32, (rows, channels), 0)
            before = jnp.where(row < items, 0.0, pltpu.roll(values, items, 0))
            behind = jnp.where(row >= rows - items, 0.0, pltpu.roll(values, rows - items, 0))
            taps[:, 0:channels] = before.astype(jnp.bfloat16)
            taps[:, channels : 2 * channels] = values.astype(jnp.bfloat16)
            taps[:, 2 * channels : 3 * channels] = behind.astype(jnp.bfloat16)
        return jnp.dot(taps[...], kernels[layer], preferred_element_type=jnp.float32)

    ones = jnp.ones((channels, LANES), jnp.bfloat16)
    start = in_ref[...]
    middle = conv(silu(layer_norm(start, ones)), 0).astype(jnp.bfloat16)
    after = (start.astype(jnp.float32) + conv(silu(layer_norm(middle, ones)), 1)).astype(jnp.bfloat16)

    normed = layer_norm(after, ones).astype(jnp.bfloat16)
    taps[...] = jnp.dot(normed, packed[...], preferred_element_type=jnp.float32).astype(jnp.bfloat16)
    queries = taps[:, 0:channels]
    keys = taps[:, channels : 2 * channels]
    values = taps[:, 2 * channels : 3 * channels]

    head_size = channels // HEADS
    block = 16 if aligned else items
    size = frames * block
    apart = within((size, size), 0, block) != within((size, size), 1, block)
    blocked = jnp.where(apart, -1e30, 0.0)
    scale = head_size ** (-0.5) * LOG2_E
    groups = [(first, min(first + LANES, channels)) for first in range(0, channels, LANES)]
    tall = jnp.ones((size, LANES), jnp.bfloat16)

    def part(whole, first):
        if block == items:
            return whole
        return jnp.concatenate(
            [whole[f * items + first : f * items + first + block] for f in range(frames)], axis=0
        )

    mixed_blocks = []
    for first in range(0, items, block):
        q, k, v = part(queries, first), part(keys, first), part(values, first)
        mixed = []
        for low, high in groups:
            heads = (high - low) // head_size
            owner = bucket((size, high - low), 1, head_size)
            chosen = q[:, low:high]
            if heads > 1:
                chosen = jnp.concatenate(
                    [jnp.where(owner == head, chosen, jnp.zeros_like(chosen)) for head in range(heads)], axis=0
                )
            scores = lax.dot_general(
                chosen, k[:, low:high], (((1,), (1,)), ((), ())), preferred_element_type=jnp.float32
            )
            scores = scores.reshape(heads, size, size) * scale + blocked
            top = jnp.max(scores, axis=-1, keepdims=True)
            raised = jnp.exp2(scores - top).astype(jnp.bfloat16).reshape(heads * size, size)
            both = jnp.dot(raised, jnp.concatenate([tall, v[:, low:high]], axis=1), preferred_element_type=jnp.float32)
            share = both[:, LANES:] / both[:, : high - low]
            out = share[0:size]
            for head in range(1, heads):
                out = jnp.where(owner == head, share[head * size : (head + 1) * size], out)
            mixed.append(out.astype(jnp.bfloat16))
        mixed_blocks.append(jnp.concatenate(mixed, axis=1))
    if len(mixed_blocks) == 1:
        mixed = mixed_blocks[0]
    else:
        mixed = jnp.concatenate(
            [piece[f * block : (f + 1) * block] for f in range(frames) for piece in mixed_blocks], axis=0
        )
    result = after.astype(jnp.float32) + jnp.dot(mixed, outward[...], preferred_element_type=jnp.float32)
    out_ref[...] = result.astype(jnp.bfloat16)


def temporal_part(frames, items, values, kernels, packed, outward):
    rows, channels = values.shape
    kernels = kernels.reshape(2, 3 * channels, kernels.shape[-1])
    resident = pl.BlockSpec(memory_space=pltpu.VMEM)
    return pl.pallas_call(
        functools.partial(temporal_kernel, frames, items),
        out_shape=jax.ShapeDtypeStruct((rows, channels), jnp.bfloat16),
        in_specs=[resident] * 4,
        out_specs=pl.BlockSpec(memory_space=pltpu.VMEM),
        scratch_shapes=[
            pltpu.VMEM((rows, 3 * channels), jnp.bfloat16),
        ],
        compiler_params=pltpu.CompilerParams(vmem_limit_bytes=24 * MIB),
    )(values, kernels, packed, outward)


def assemble_kernel(*refs):
    *parts, out_ref, sems = refs
    copies = [pltpu.make_async_copy(part, out_ref.at[i], sems.at[i]) for i, part in enumerate(parts)]
    for copy in copies:
        copy.start()
    for copy in copies:
        copy.wait()


def assembled(parts):
    return pl.pallas_call(
        assemble_kernel,
        out_shape=jax.ShapeDtypeStruct((len(parts),) + parts[0].shape, parts[0].dtype),
        in_specs=[pl.BlockSpec(memory_space=pl.ANY)] * len(parts),
        out_specs=pl.BlockSpec(memory_space=pl.ANY),
        scratch_shapes=[pltpu.SemaphoreType.DMA((len(parts),))],
        compiler_params=pltpu.CompilerParams(vmem_limit_bytes=MIB),
    )(*parts)


def shards(incoming, plan, waiting, spatial_weight, temporal_weight, attn_in, attn_out):
    clips, _, height, width, channels = incoming.shape
    cells = height * width
    devices = lax.axis_size("seq")
    share = cells // devices
    sections = lax.axis_size("section")
    entering = incoming.reshape(clips, cells, channels)
    current = waiting.reshape(cells, channels)
    collected = []
    for tick in range(TICKS):
        if tick == 0:
            after = spatial_part(height, width, current, spatial_weight[0])
        else:
            ring = [(i, (i + 1) % sections) for i in range(sections)]
            passed = lax.ppermute(current, "section", ring)
            after = spatial_part(height, width, passed, spatial_weight[0], plan, entering, tick - 1)
        grouped = after.reshape(devices, share, channels)
        gathered = lax.all_to_all(grouped, "seq", split_axis=0, concat_axis=0, tiled=True)
        done = temporal_part(
            devices, share, gathered.reshape(devices * share, channels), temporal_weight[0], attn_in[0], attn_out[0]
        )
        back = lax.all_to_all(
            done.reshape(devices, share, channels), "seq", split_axis=0, concat_axis=0, tiled=True
        )
        current = back.reshape(cells, channels)
        collected.append(current)
    return assembled(collected).reshape(TICKS, 1, 1, height, width, channels)


def solution(mesh):
    return jax.shard_map(
        shards,
        mesh=mesh,
        in_specs=(
            P(None, "seq", None, None, None),
            P(),
            P("section", "seq", None, None, None),
            P("section", None, None, None, None),
            P("section", None, None, None, None),
            P("section", None, None),
            P("section", None, None),
        ),
        out_specs=P(None, "section", "seq", None, None, None),
        check_vma=False,
    )
```

```python
import functools

import jax
import jax.numpy as jnp
from jax import lax
from jax.experimental import pallas as pl
from jax.experimental.pallas import tpu as pltpu
from jax.sharding import PartitionSpec as P

HEADS = 5
GROUPS = 32
TICKS = 3
EPSILON = 1e-05
MIB = 1 << 20
LANES = 128
LOG2_E = 1.4426950408889634


def silu(values):
    half = 0.5 * values
    return half + half * jnp.tanh(half)


def bucket(shape, dim, size):
    index = lax.broadcasted_iota(jnp.int32, shape, dim).astype(jnp.float32)
    return jnp.floor((index + 0.5) * (1.0 / size))


def within(shape, dim, size):
    index = lax.broadcasted_iota(jnp.int32, shape, dim).astype(jnp.float32)
    return index - size * jnp.floor((index + 0.5) * (1.0 / size))


def chunk_shape(share, channels):
    if share % 16 == 0 and channels % LANES * 2 == LANES:
        return (share * channels // LANES, LANES)
    return (share, channels)


def pack(out_ref, values):
    devices, height, width = out_ref.shape
    rows, channels = values.shape
    share = rows // devices
    if width == channels:
        out_ref[...] = values.astype(jnp.bfloat16).reshape(out_ref.shape)
        return
    columns = channels // LANES
    for device in range(devices):
        own = values[device * share : (device + 1) * share]
        for column in range(columns):
            piece = own[:, column * LANES : (column + 1) * LANES]
            out_ref[device, column * share : (column + 1) * share, :] = piece.astype(jnp.bfloat16)
        last = own[:, columns * LANES :]
        piece = jnp.concatenate([last[: share // 2], last[share // 2 :]], axis=1)
        out_ref[device, columns * share :, :] = piece.astype(jnp.bfloat16)


def unpack(in_ref, channels):
    devices, height, width = in_ref.shape
    if width == channels:
        return in_ref[...].astype(jnp.float32).reshape(devices * height, channels)
    share = height * width // channels
    columns = channels // LANES
    rows = []
    for device in range(devices):
        pieces = [
            in_ref[device, column * share : (column + 1) * share, :].astype(jnp.float32) for column in range(columns)
        ]
        last = in_ref[device, columns * share :, :].astype(jnp.float32)
        pieces.append(jnp.concatenate([last[:, : LANES // 2], last[:, LANES // 2 :]], axis=0))
        rows.append(jnp.concatenate(pieces, axis=1))
    return jnp.concatenate(rows, axis=0)


def group_total(partial, same_group):
    high = partial.astype(jnp.bfloat16).astype(jnp.float32)
    rest = partial - high
    middle = rest.astype(jnp.bfloat16).astype(jnp.float32)
    low = rest - middle
    rows = jnp.concatenate([high, middle, low, jnp.zeros_like(low)], axis=0).astype(jnp.bfloat16)
    sums = jnp.dot(rows, same_group, preferred_element_type=jnp.float32)
    return jnp.sum(sums, axis=0, keepdims=True)


def group_norm(values, same_group):
    cells, channels = values.shape
    scale = 1.0 / (cells * (channels // GROUPS))
    center = group_total(jnp.sum(values.reshape(-1, 8, channels), axis=0), same_group) * scale
    shifted = values - center
    spread = group_total(jnp.sum(jnp.square(shifted).reshape(-1, 8, channels), axis=0), same_group) * scale
    return shifted * lax.rsqrt(spread + EPSILON)


def layer_norm(values, ones):
    channels = values.shape[-1]

    def across(sums):
        pieces = -(-channels // sums.shape[-1])
        return jnp.concatenate([sums] * pieces, axis=-1)[:, :channels]

    floats = values.astype(jnp.float32)
    center = jnp.dot(values, ones, preferred_element_type=jnp.float32) * (1.0 / channels)
    shifted = floats - across(center)
    squares = jnp.square(shifted).astype(jnp.bfloat16)
    spread = jnp.dot(squares, ones, preferred_element_type=jnp.float32) * (1.0 / channels)
    return shifted * across(lax.rsqrt(spread + EPSILON))


def spatial_kernel(height, width, picks, stream, *refs):
    if picks:
        _, entering_ref, *refs = refs
    passed_ref, weight_ref, out_ref, taps, *refs = refs
    cells, channels = height * width, weight_ref.shape[-1]
    copies = []
    kernels = weight_ref
    if stream:
        kernels, sems = refs
        for layer in range(2):
            for row in range(3):
                copy = pltpu.make_async_copy(
                    weight_ref.at[layer, row], kernels.at[layer, row], sems.at[layer, row]
                )
                copy.start()
                copies.append(copy)
    edge = jnp.zeros((width, 3 * channels), jnp.bfloat16)
    taps[0:width, :] = edge
    taps[width + cells : 2 * width + cells, :] = edge
    same_group = (
        bucket((channels, channels), 0, channels // GROUPS)
        == bucket((channels, channels), 1, channels // GROUPS)
    ).astype(jnp.float32).astype(jnp.bfloat16)
    column = lax.broadcasted_iota(jnp.int32, (1, width, channels), 1)

    def conv(values, layer):
        framed = values.reshape(height, width, channels)
        left = jnp.where(column == 0, 0.0, pltpu.roll(framed, 1, 1)).reshape(cells, channels)
        right = jnp.where(column == width - 1, 0.0, pltpu.roll(framed, width - 1, 1)).reshape(cells, channels)
        taps[width : width + cells, 0:channels] = left.astype(jnp.bfloat16)
        taps[width : width + cells, channels : 2 * channels] = values.astype(jnp.bfloat16)
        taps[width : width + cells, 2 * channels : 3 * channels] = right.astype(jnp.bfloat16)
        total = None
        for row in range(3):
            if stream:
                copies[3 * layer + row].wait()
            part = jnp.dot(
                taps[row * width : row * width + cells, :],
                kernels[layer, row],
                preferred_element_type=jnp.float32,
            )
            total = part if total is None else total + part
        return total

    if picks:
        entering = entering_ref[...].astype(jnp.float32)
        start = jnp.where(lax.axis_index("section") == 0, entering, unpack(passed_ref, channels))
    else:
        start = passed_ref[...].astype(jnp.float32)
    middle = conv(silu(group_norm(start, same_group)), 0).astype(jnp.bfloat16).astype(jnp.float32)
    after = conv(silu(group_norm(middle, same_group)), 1)
    pack(out_ref, start + after)


def spatial_part(height, width, devices, passed, weights, plan=None, entering=None, turn=0):
    cells, channels = height * width, weights.shape[-1]
    chunks = (devices,) + chunk_shape(cells // devices, channels)
    weights = weights.reshape(2, 3, 3 * channels, weights.shape[-1])
    stream = plan is None
    specs = [
        pl.BlockSpec(passed.shape, lambda i, *_: (0,) * passed.ndim),
        pl.BlockSpec(memory_space=pltpu.HBM if stream else pltpu.VMEM),
    ]
    operands = [passed, weights]
    if plan is not None:
        specs = [pl.BlockSpec((None, cells, channels), lambda i, order: (order[turn], 0, 0))] + specs
        operands = [plan, entering] + operands
    return pl.pallas_call(
        functools.partial(spatial_kernel, height, width, plan is not None, stream),
        out_shape=jax.ShapeDtypeStruct(chunks, jnp.bfloat16),
        grid_spec=pltpu.PrefetchScalarGridSpec(
            num_scalar_prefetch=0 if plan is None else 1,
            grid=(1,),
            in_specs=specs,
            out_specs=pl.BlockSpec(chunks, lambda i, *_: (0, 0, 0)),
            scratch_shapes=[pltpu.VMEM((cells + 2 * width, 3 * channels), jnp.bfloat16)]
            + ([pltpu.VMEM(weights.shape, jnp.bfloat16), pltpu.SemaphoreType.DMA((2, 3))] if stream else []),
        ),
        compiler_params=pltpu.CompilerParams(vmem_limit_bytes=(52 if stream else 24) * MIB),
    )(*operands)


def temporal_kernel(frames, items, in_ref, kernels, packed, outward, out_ref, taps):
    rows, channels = frames * items, outward.shape[-1]
    aligned = items % 16 == 0

    def conv(values, layer):
        if aligned:
            whole = values.astype(jnp.bfloat16)
            edge = jnp.zeros((items, channels), jnp.bfloat16)
            taps[0:items, 0:channels] = edge
            taps[items:rows, 0:channels] = whole[0 : rows - items]
            taps[:, channels : 2 * channels] = whole
            taps[0 : rows - items, 2 * channels : 3 * channels] = whole[items:rows]
            taps[rows - items : rows, 2 * channels : 3 * channels] = edge
        else:
            row = lax.broadcasted_iota(jnp.int32, (rows, channels), 0)
            before = jnp.where(row < items, 0.0, pltpu.roll(values, items, 0))
            behind = jnp.where(row >= rows - items, 0.0, pltpu.roll(values, rows - items, 0))
            taps[:, 0:channels] = before.astype(jnp.bfloat16)
            taps[:, channels : 2 * channels] = values.astype(jnp.bfloat16)
            taps[:, 2 * channels : 3 * channels] = behind.astype(jnp.bfloat16)
        return jnp.dot(taps[...], kernels[layer], preferred_element_type=jnp.float32)

    ones = jnp.ones((channels, LANES), jnp.bfloat16)
    start = unpack(in_ref, channels)
    middle = conv(silu(layer_norm(start.astype(jnp.bfloat16), ones)), 0).astype(jnp.bfloat16)
    after = (start + conv(silu(layer_norm(middle, ones)), 1)).astype(jnp.bfloat16)

    normed = layer_norm(after, ones).astype(jnp.bfloat16)
    taps[...] = jnp.dot(normed, packed[...], preferred_element_type=jnp.float32).astype(jnp.bfloat16)
    queries = taps[:, 0:channels]
    keys = taps[:, channels : 2 * channels]
    values = taps[:, 2 * channels : 3 * channels]

    head_size = channels // HEADS
    block = 16 if aligned else items
    size = frames * block
    apart = within((size, size), 0, block) != within((size, size), 1, block)
    blocked = jnp.where(apart, -1e30, 0.0)
    scale = head_size ** (-0.5) * LOG2_E
    groups = [(first, min(first + LANES, channels)) for first in range(0, channels, LANES)]
    tall = jnp.ones((size, LANES), jnp.bfloat16)

    def part(whole, first):
        if block == items:
            return whole
        return jnp.concatenate(
            [whole[f * items + first : f * items + first + block] for f in range(frames)], axis=0
        )

    mixed_blocks = []
    for first in range(0, items, block):
        q, k, v = part(queries, first), part(keys, first), part(values, first)
        mixed = []
        for low, high in groups:
            heads = (high - low) // head_size
            owner = bucket((size, high - low), 1, head_size)
            chosen = q[:, low:high]
            if heads > 1:
                chosen = jnp.concatenate(
                    [jnp.where(owner == head, chosen, jnp.zeros_like(chosen)) for head in range(heads)], axis=0
                )
            scores = lax.dot_general(
                chosen, k[:, low:high], (((1,), (1,)), ((), ())), preferred_element_type=jnp.float32
            )
            scores = scores.reshape(heads, size, size) * scale + blocked
            top = jnp.max(scores, axis=-1, keepdims=True)
            raised = jnp.exp2(scores - top).astype(jnp.bfloat16).reshape(heads * size, size)
            both = jnp.dot(raised, jnp.concatenate([tall, v[:, low:high]], axis=1), preferred_element_type=jnp.float32)
            share = both[:, LANES:] / both[:, : high - low]
            out = share[0:size]
            for head in range(1, heads):
                out = jnp.where(owner == head, share[head * size : (head + 1) * size], out)
            mixed.append(out.astype(jnp.bfloat16))
        mixed_blocks.append(jnp.concatenate(mixed, axis=1))
    if len(mixed_blocks) == 1:
        mixed = mixed_blocks[0]
    else:
        mixed = jnp.concatenate(
            [piece[f * block : (f + 1) * block] for f in range(frames) for piece in mixed_blocks], axis=0
        )
    result = after.astype(jnp.float32) + jnp.dot(mixed, outward[...], preferred_element_type=jnp.float32)
    pack(out_ref, result)


def temporal_part(frames, items, values, kernels, packed, outward):
    rows, channels = frames * items, outward.shape[-1]
    kernels = kernels.reshape(2, 3 * channels, kernels.shape[-1])
    resident = pl.BlockSpec(memory_space=pltpu.VMEM)
    return pl.pallas_call(
        functools.partial(temporal_kernel, frames, items),
        out_shape=jax.ShapeDtypeStruct(values.shape, jnp.bfloat16),
        in_specs=[resident] * 4,
        out_specs=pl.BlockSpec(memory_space=pltpu.VMEM),
        scratch_shapes=[
            pltpu.VMEM((rows, 3 * channels), jnp.bfloat16),
        ],
        compiler_params=pltpu.CompilerParams(vmem_limit_bytes=24 * MIB),
    )(values, kernels, packed, outward)


def collect_kernel(tick, *refs):
    in_ref, *_, out_ref, rows, sem = refs
    rows[...] = unpack(in_ref, rows.shape[-1]).astype(jnp.bfloat16)
    copy = pltpu.make_async_copy(rows, out_ref.at[tick], sem)
    copy.start()
    copy.wait()


def collect(tick, values, shape, outputs=None):
    before = [] if outputs is None else [outputs]
    return pl.pallas_call(
        functools.partial(collect_kernel, tick),
        out_shape=jax.ShapeDtypeStruct(shape, values.dtype),
        in_specs=[pl.BlockSpec(memory_space=pltpu.VMEM)] + [pl.BlockSpec(memory_space=pl.ANY)] * len(before),
        out_specs=pl.BlockSpec(memory_space=pl.ANY),
        scratch_shapes=[pltpu.VMEM(shape[1:], values.dtype), pltpu.SemaphoreType.DMA],
        input_output_aliases={1: 0} if before else {},
        compiler_params=pltpu.CompilerParams(vmem_limit_bytes=4 * MIB),
        cost_estimate=pl.CostEstimate(flops=0, bytes_accessed=4 * values.size, transcendentals=0),
    )(values, *before)


def shards(incoming, plan, waiting, spatial_weight, temporal_weight, attn_in, attn_out):
    clips, _, height, width, channels = incoming.shape
    cells = height * width
    devices = lax.axis_size("seq")
    share = cells // devices
    sections = lax.axis_size("section")
    entering = incoming.reshape(clips, cells, channels)
    current = waiting.reshape(cells, channels)
    ring = [(i, (i + 1) % sections) for i in range(sections)]
    outputs = None
    for tick in range(TICKS):
        if tick == 0:
            after = spatial_part(height, width, devices, current, spatial_weight[0])
        else:
            passed = lax.ppermute(current, "section", ring)
            after = spatial_part(height, width, devices, passed, spatial_weight[0], plan, entering, tick - 1)
        gathered = lax.all_to_all(after, "seq", split_axis=0, concat_axis=0, tiled=True)
        done = temporal_part(devices, share, gathered, temporal_weight[0], attn_in[0], attn_out[0])
        current = lax.all_to_all(done, "seq", split_axis=0, concat_axis=0, tiled=True)
        outputs = collect(tick, current, (TICKS, cells, channels), outputs)
    return outputs.reshape(TICKS, 1, 1, height, width, channels)


def solution(mesh):
    return jax.shard_map(
        shards,
        mesh=mesh,
        in_specs=(
            P(None, "seq", None, None, None),
            P(),
            P("section", "seq", None, None, None),
            P("section", None, None, None, None),
            P("section", None, None, None, None),
            P("section", None, None),
            P("section", None, None),
        ),
        out_specs=P(None, "section", "seq", None, None, None),
        check_vma=False,
    )
```

```python
import functools

import jax
import jax.numpy as jnp
from jax import lax
from jax.experimental import pallas as pl
from jax.experimental.pallas import tpu as pltpu
from jax.sharding import PartitionSpec as P

HEADS = 5
GROUPS = 32
TICKS = 3
EPSILON = 1e-05
MIB = 1 << 20
LANES = 128
LOG2_E = 1.4426950408889634


def silu(values):
    half = 0.5 * values
    return half + half * jnp.tanh(half)


def bucket(shape, dim, size):
    index = lax.broadcasted_iota(jnp.int32, shape, dim).astype(jnp.float32)
    return jnp.floor((index + 0.5) * (1.0 / size))


def within(shape, dim, size):
    index = lax.broadcasted_iota(jnp.int32, shape, dim).astype(jnp.float32)
    return index - size * jnp.floor((index + 0.5) * (1.0 / size))


def chunk_shape(share, channels):
    if share % 16 == 0 and channels % LANES * 2 == LANES:
        return (share * channels // LANES, LANES)
    return (share, channels)


def pack(out_ref, values):
    devices, height, width = out_ref.shape
    rows, channels = values.shape
    share = rows // devices
    if width == channels:
        out_ref[...] = values.astype(jnp.bfloat16).reshape(out_ref.shape)
        return
    columns = channels // LANES
    for device in range(devices):
        own = values[device * share : (device + 1) * share]
        for column in range(columns):
            piece = own[:, column * LANES : (column + 1) * LANES]
            out_ref[device, column * share : (column + 1) * share, :] = piece.astype(jnp.bfloat16)
        last = own[:, columns * LANES :]
        piece = jnp.concatenate([last[: share // 2], last[share // 2 :]], axis=1)
        out_ref[device, columns * share :, :] = piece.astype(jnp.bfloat16)


def unpack(in_ref, channels):
    devices, height, width = in_ref.shape
    if width == channels:
        return in_ref[...].astype(jnp.float32).reshape(devices * height, channels)
    share = height * width // channels
    columns = channels // LANES
    rows = []
    for device in range(devices):
        pieces = [
            in_ref[device, column * share : (column + 1) * share, :].astype(jnp.float32) for column in range(columns)
        ]
        last = in_ref[device, columns * share :, :].astype(jnp.float32)
        pieces.append(jnp.concatenate([last[:, : LANES // 2], last[:, LANES // 2 :]], axis=0))
        rows.append(jnp.concatenate(pieces, axis=1))
    return jnp.concatenate(rows, axis=0)


def group_total(partial, same_group):
    high = partial.astype(jnp.bfloat16).astype(jnp.float32)
    rest = partial - high
    middle = rest.astype(jnp.bfloat16).astype(jnp.float32)
    low = rest - middle
    rows = jnp.concatenate([high, middle, low, jnp.zeros_like(low)], axis=0).astype(jnp.bfloat16)
    sums = jnp.dot(rows, same_group, preferred_element_type=jnp.float32)
    return jnp.sum(sums, axis=0, keepdims=True)


def group_norm(values, same_group):
    cells, channels = values.shape
    scale = 1.0 / (cells * (channels // GROUPS))
    center = group_total(jnp.sum(values.reshape(-1, 8, channels), axis=0), same_group) * scale
    shifted = values - center
    spread = group_total(jnp.sum(jnp.square(shifted).reshape(-1, 8, channels), axis=0), same_group) * scale
    return shifted * lax.rsqrt(spread + EPSILON)


def layer_norm(values, ones):
    channels = values.shape[-1]

    def across(sums):
        pieces = -(-channels // sums.shape[-1])
        return jnp.concatenate([sums] * pieces, axis=-1)[:, :channels]

    floats = values.astype(jnp.float32)
    center = jnp.dot(values, ones, preferred_element_type=jnp.float32) * (1.0 / channels)
    shifted = floats - across(center)
    squares = jnp.square(shifted).astype(jnp.bfloat16)
    spread = jnp.dot(squares, ones, preferred_element_type=jnp.float32) * (1.0 / channels)
    return shifted * across(lax.rsqrt(spread + EPSILON))


def spatial_kernel(height, width, picks, stream, *refs):
    if picks:
        _, entering_ref, *refs = refs
    if stream:
        passed_ref, weight_ref, later_ref, out_ref, held_ref, taps, kernels, sems = refs
    else:
        passed_ref, weight_ref, out_ref, taps = refs
        kernels = weight_ref
    cells, channels = height * width, weight_ref.shape[-1]
    copies = []
    if stream:
        pairs = [(weight_ref.at[layer, row], kernels.at[layer, row]) for layer in range(2) for row in range(3)]
        pairs.append((later_ref, held_ref))
        copies = [pltpu.make_async_copy(source, target, sems.at[i]) for i, (source, target) in enumerate(pairs)]
        for copy in copies:
            copy.start()
    edge = jnp.zeros((width, 3 * channels), jnp.bfloat16)
    taps[0:width, :] = edge
    taps[width + cells : 2 * width + cells, :] = edge
    same_group = (
        bucket((channels, channels), 0, channels // GROUPS)
        == bucket((channels, channels), 1, channels // GROUPS)
    ).astype(jnp.float32).astype(jnp.bfloat16)
    column = lax.broadcasted_iota(jnp.int32, (1, width, channels), 1)

    def conv(values, layer):
        framed = values.reshape(height, width, channels)
        left = jnp.where(column == 0, 0.0, pltpu.roll(framed, 1, 1)).reshape(cells, channels)
        right = jnp.where(column == width - 1, 0.0, pltpu.roll(framed, width - 1, 1)).reshape(cells, channels)
        taps[width : width + cells, 0:channels] = left.astype(jnp.bfloat16)
        taps[width : width + cells, channels : 2 * channels] = values.astype(jnp.bfloat16)
        taps[width : width + cells, 2 * channels : 3 * channels] = right.astype(jnp.bfloat16)
        total = None
        for row in range(3):
            if stream:
                copies[3 * layer + row].wait()
            part = jnp.dot(
                taps[row * width : row * width + cells, :],
                kernels[layer, row],
                preferred_element_type=jnp.float32,
            )
            total = part if total is None else total + part
        return total

    if picks:
        entering = entering_ref[...].astype(jnp.float32)
        start = jnp.where(lax.axis_index("section") == 0, entering, unpack(passed_ref, channels))
    else:
        start = passed_ref[...].astype(jnp.float32)
    middle = conv(silu(group_norm(start, same_group)), 0).astype(jnp.bfloat16).astype(jnp.float32)
    after = conv(silu(group_norm(middle, same_group)), 1)
    pack(out_ref, start + after)
    if stream:
        copies[-1].wait()


def spatial_part(height, width, devices, passed, weights, plan=None, entering=None, turn=0, later=None):
    cells, channels = height * width, weights.shape[-1]
    chunks = (devices,) + chunk_shape(cells // devices, channels)
    weights = weights.reshape(2, 3, 3 * channels, weights.shape[-1])
    stream = plan is None
    specs = [
        pl.BlockSpec(passed.shape, lambda i, *_: (0,) * passed.ndim),
        pl.BlockSpec(memory_space=pltpu.HBM if stream else pltpu.VMEM),
    ]
    operands = [passed, weights]
    if plan is not None:
        specs = [pl.BlockSpec((None, cells, channels), lambda i, order: (order[turn], 0, 0))] + specs
        operands = [plan, entering] + operands
    out_shape = jax.ShapeDtypeStruct(chunks, jnp.bfloat16)
    out_specs = pl.BlockSpec(chunks, lambda i, *_: (0, 0, 0))
    if stream:
        specs.append(pl.BlockSpec(memory_space=pltpu.HBM))
        operands.append(later)
        out_shape = [out_shape, jax.ShapeDtypeStruct(later.shape, later.dtype)]
        out_specs = [out_specs, pl.BlockSpec(memory_space=pltpu.VMEM)]
    return pl.pallas_call(
        functools.partial(spatial_kernel, height, width, plan is not None, stream),
        out_shape=out_shape,
        grid_spec=pltpu.PrefetchScalarGridSpec(
            num_scalar_prefetch=0 if plan is None else 1,
            grid=(1,),
            in_specs=specs,
            out_specs=out_specs,
            scratch_shapes=[pltpu.VMEM((cells + 2 * width, 3 * channels), jnp.bfloat16)]
            + ([pltpu.VMEM(weights.shape, jnp.bfloat16), pltpu.SemaphoreType.DMA((7,))] if stream else []),
        ),
        compiler_params=pltpu.CompilerParams(vmem_limit_bytes=(52 if stream else 24) * MIB),
    )(*operands)


def temporal_kernel(frames, items, in_ref, kernels, packed, outward, out_ref, taps):
    rows, channels = frames * items, outward.shape[-1]
    aligned = items % 16 == 0

    def conv(values, layer):
        if aligned:
            whole = values.astype(jnp.bfloat16)
            edge = jnp.zeros((items, channels), jnp.bfloat16)
            taps[0:items, 0:channels] = edge
            taps[items:rows, 0:channels] = whole[0 : rows - items]
            taps[:, channels : 2 * channels] = whole
            taps[0 : rows - items, 2 * channels : 3 * channels] = whole[items:rows]
            taps[rows - items : rows, 2 * channels : 3 * channels] = edge
        else:
            row = lax.broadcasted_iota(jnp.int32, (rows, channels), 0)
            before = jnp.where(row < items, 0.0, pltpu.roll(values, items, 0))
            behind = jnp.where(row >= rows - items, 0.0, pltpu.roll(values, rows - items, 0))
            taps[:, 0:channels] = before.astype(jnp.bfloat16)
            taps[:, channels : 2 * channels] = values.astype(jnp.bfloat16)
            taps[:, 2 * channels : 3 * channels] = behind.astype(jnp.bfloat16)
        return jnp.dot(taps[...], kernels[layer], preferred_element_type=jnp.float32)

    ones = jnp.ones((channels, LANES), jnp.bfloat16)
    start = unpack(in_ref, channels)
    middle = conv(silu(layer_norm(start.astype(jnp.bfloat16), ones)), 0).astype(jnp.bfloat16)
    after = (start + conv(silu(layer_norm(middle, ones)), 1)).astype(jnp.bfloat16)

    normed = layer_norm(after, ones).astype(jnp.bfloat16)
    taps[...] = jnp.dot(normed, packed[...], preferred_element_type=jnp.float32).astype(jnp.bfloat16)
    queries = taps[:, 0:channels]
    keys = taps[:, channels : 2 * channels]
    values = taps[:, 2 * channels : 3 * channels]

    head_size = channels // HEADS
    block = 16 if aligned else items
    size = frames * block
    apart = within((size, size), 0, block) != within((size, size), 1, block)
    blocked = jnp.where(apart, -1e30, 0.0)
    scale = head_size ** (-0.5) * LOG2_E
    groups = [(first, min(first + LANES, channels)) for first in range(0, channels, LANES)]
    tall = jnp.ones((size, LANES), jnp.bfloat16)

    def part(whole, first):
        if block == items:
            return whole
        return jnp.concatenate(
            [whole[f * items + first : f * items + first + block] for f in range(frames)], axis=0
        )

    mixed_blocks = []
    for first in range(0, items, block):
        q, k, v = part(queries, first), part(keys, first), part(values, first)
        mixed = []
        for low, high in groups:
            heads = (high - low) // head_size
            owner = bucket((size, high - low), 1, head_size)
            chosen = q[:, low:high]
            if heads > 1:
                chosen = jnp.concatenate(
                    [jnp.where(owner == head, chosen, jnp.zeros_like(chosen)) for head in range(heads)], axis=0
                )
            scores = lax.dot_general(
                chosen, k[:, low:high], (((1,), (1,)), ((), ())), preferred_element_type=jnp.float32
            )
            scores = scores.reshape(heads, size, size) * scale + blocked
            top = jnp.max(scores, axis=-1, keepdims=True)
            raised = jnp.exp2(scores - top).astype(jnp.bfloat16).reshape(heads * size, size)
            both = jnp.dot(raised, jnp.concatenate([tall, v[:, low:high]], axis=1), preferred_element_type=jnp.float32)
            share = both[:, LANES:] / both[:, : high - low]
            out = share[0:size]
            for head in range(1, heads):
                out = jnp.where(owner == head, share[head * size : (head + 1) * size], out)
            mixed.append(out.astype(jnp.bfloat16))
        mixed_blocks.append(jnp.concatenate(mixed, axis=1))
    if len(mixed_blocks) == 1:
        mixed = mixed_blocks[0]
    else:
        mixed = jnp.concatenate(
            [piece[f * block : (f + 1) * block] for f in range(frames) for piece in mixed_blocks], axis=0
        )
    result = after.astype(jnp.float32) + jnp.dot(mixed, outward[...], preferred_element_type=jnp.float32)
    pack(out_ref, result)


def temporal_part(frames, items, values, kernels, packed, outward):
    rows, channels = frames * items, outward.shape[-1]
    kernels = kernels.reshape(2, 3 * channels, kernels.shape[-1])
    resident = pl.BlockSpec(memory_space=pltpu.VMEM)
    return pl.pallas_call(
        functools.partial(temporal_kernel, frames, items),
        out_shape=jax.ShapeDtypeStruct(values.shape, jnp.bfloat16),
        in_specs=[resident] * 4,
        out_specs=pl.BlockSpec(memory_space=pltpu.VMEM),
        scratch_shapes=[
            pltpu.VMEM((rows, 3 * channels), jnp.bfloat16),
        ],
        compiler_params=pltpu.CompilerParams(vmem_limit_bytes=24 * MIB),
    )(values, kernels, packed, outward)


def collect_kernel(tick, *refs):
    in_ref, *_, out_ref, rows, sem = refs
    rows[...] = unpack(in_ref, rows.shape[-1]).astype(jnp.bfloat16)
    copy = pltpu.make_async_copy(rows, out_ref.at[tick], sem)
    copy.start()
    copy.wait()


def collect(tick, values, shape, outputs=None):
    before = [] if outputs is None else [outputs]
    return pl.pallas_call(
        functools.partial(collect_kernel, tick),
        out_shape=jax.ShapeDtypeStruct(shape, values.dtype),
        in_specs=[pl.BlockSpec(memory_space=pltpu.VMEM)] + [pl.BlockSpec(memory_space=pl.ANY)] * len(before),
        out_specs=pl.BlockSpec(memory_space=pl.ANY),
        scratch_shapes=[pltpu.VMEM(shape[1:], values.dtype), pltpu.SemaphoreType.DMA],
        input_output_aliases={1: 0} if before else {},
        compiler_params=pltpu.CompilerParams(vmem_limit_bytes=4 * MIB),
        cost_estimate=pl.CostEstimate(flops=0, bytes_accessed=4 * values.size, transcendentals=0),
    )(values, *before)


def shards(incoming, plan, waiting, spatial_weight, temporal_weight, attn_in, attn_out):
    clips, _, height, width, channels = incoming.shape
    cells = height * width
    devices = lax.axis_size("seq")
    share = cells // devices
    sections = lax.axis_size("section")
    entering = incoming.reshape(clips, cells, channels)
    current = waiting.reshape(cells, channels)
    ring = [(i, (i + 1) % sections) for i in range(sections)]
    outputs = None
    for tick in range(TICKS):
        if tick == 0:
            after, temporal = spatial_part(height, width, devices, current, spatial_weight[0], later=temporal_weight[0])
        else:
            passed, outputs = lax.optimization_barrier((lax.ppermute(current, "section", ring), outputs))
            after = spatial_part(height, width, devices, passed, spatial_weight[0], plan, entering, tick - 1)
        gathered = lax.all_to_all(after, "seq", split_axis=0, concat_axis=0, tiled=True)
        done = temporal_part(devices, share, gathered, temporal, attn_in[0], attn_out[0])
        current = lax.all_to_all(done, "seq", split_axis=0, concat_axis=0, tiled=True)
        outputs = collect(tick, current, (TICKS, cells, channels), outputs)
    return outputs.reshape(TICKS, 1, 1, height, width, channels)


def solution(mesh):
    return jax.shard_map(
        shards,
        mesh=mesh,
        in_specs=(
            P(None, "seq", None, None, None),
            P(),
            P("section", "seq", None, None, None),
            P("section", None, None, None, None),
            P("section", None, None, None, None),
            P("section", None, None),
            P("section", None, None),
        ),
        out_specs=P(None, "section", "seq", None, None, None),
        check_vma=False,
    )
```

```python
import functools

import jax
import jax.numpy as jnp
from jax import lax
from jax.experimental import pallas as pl
from jax.experimental.pallas import tpu as pltpu
from jax.sharding import PartitionSpec as P

HEADS = 5
GROUPS = 32
TICKS = 3
EPSILON = 1e-05
MIB = 1 << 20
LANES = 128
LOG2_E = 1.4426950408889634


def silu(values):
    half = 0.5 * values
    return half + half * jnp.tanh(half)


def bucket(shape, dim, size):
    index = lax.broadcasted_iota(jnp.int32, shape, dim).astype(jnp.float32)
    return jnp.floor((index + 0.5) * (1.0 / size))


def within(shape, dim, size):
    index = lax.broadcasted_iota(jnp.int32, shape, dim).astype(jnp.float32)
    return index - size * jnp.floor((index + 0.5) * (1.0 / size))


def chunk_shape(share, channels):
    if share % 16 == 0 and channels % LANES * 2 == LANES:
        return (share * channels // LANES, LANES)
    return (share, channels)


def pack(out_ref, values):
    devices, height, width = out_ref.shape
    rows, channels = values.shape
    share = rows // devices
    if width == channels:
        out_ref[...] = values.astype(jnp.bfloat16).reshape(out_ref.shape)
        return
    columns = channels // LANES
    for device in range(devices):
        own = values[device * share : (device + 1) * share]
        for column in range(columns):
            piece = own[:, column * LANES : (column + 1) * LANES]
            out_ref[device, column * share : (column + 1) * share, :] = piece.astype(jnp.bfloat16)
        last = own[:, columns * LANES :]
        piece = jnp.concatenate([last[: share // 2], last[share // 2 :]], axis=1)
        out_ref[device, columns * share :, :] = piece.astype(jnp.bfloat16)


def unpack(in_ref, channels):
    devices, height, width = in_ref.shape
    if width == channels:
        return in_ref[...].astype(jnp.float32).reshape(devices * height, channels)
    share = height * width // channels
    columns = channels // LANES
    rows = []
    for device in range(devices):
        pieces = [
            in_ref[device, column * share : (column + 1) * share, :].astype(jnp.float32) for column in range(columns)
        ]
        last = in_ref[device, columns * share :, :].astype(jnp.float32)
        pieces.append(jnp.concatenate([last[:, : LANES // 2], last[:, LANES // 2 :]], axis=0))
        rows.append(jnp.concatenate(pieces, axis=1))
    return jnp.concatenate(rows, axis=0)


def group_total(partial, same_group):
    high = partial.astype(jnp.bfloat16).astype(jnp.float32)
    rest = partial - high
    middle = rest.astype(jnp.bfloat16).astype(jnp.float32)
    low = rest - middle
    rows = jnp.concatenate([high, middle, low, jnp.zeros_like(low)], axis=0).astype(jnp.bfloat16)
    sums = jnp.dot(rows, same_group, preferred_element_type=jnp.float32)
    return jnp.sum(sums, axis=0, keepdims=True)


def group_norm(values, same_group):
    cells, channels = values.shape
    scale = 1.0 / (cells * (channels // GROUPS))
    partial = jnp.sum(values.reshape(-1, 8, channels), axis=0)
    center = group_total(partial, same_group) * scale
    own = jnp.sum(partial, axis=0, keepdims=True) * (1.0 / cells)
    squares = jnp.sum(jnp.square(values - own).reshape(-1, 8, channels), axis=0)
    squares = squares + jnp.square(own - center) * (cells / 8)
    spread = group_total(squares, same_group) * scale
    return (values - center) * lax.rsqrt(spread + EPSILON)


def layer_norm(values, ones):
    channels = values.shape[-1]

    def across(sums):
        pieces = -(-channels // sums.shape[-1])
        return jnp.concatenate([sums] * pieces, axis=-1)[:, :channels]

    floats = values.astype(jnp.float32)
    center = jnp.dot(values, ones, preferred_element_type=jnp.float32) * (1.0 / channels)
    shifted = floats - across(center)
    squares = jnp.square(shifted).astype(jnp.bfloat16)
    spread = jnp.dot(squares, ones, preferred_element_type=jnp.float32) * (1.0 / channels)
    return shifted * across(lax.rsqrt(spread + EPSILON))


def spatial_kernel(height, width, picks, stream, *refs):
    if picks:
        _, entering_ref, *refs = refs
    if stream:
        passed_ref, weight_ref, later_ref, out_ref, held_ref, taps, kernels, sems = refs
    else:
        passed_ref, weight_ref, out_ref, taps = refs
        kernels = weight_ref
    cells, channels = height * width, weight_ref.shape[-1]
    copies = []
    if stream:
        pairs = [(weight_ref.at[layer, row], kernels.at[layer, row]) for layer in range(2) for row in range(3)]
        pairs.append((later_ref, held_ref))
        copies = [pltpu.make_async_copy(source, target, sems.at[i]) for i, (source, target) in enumerate(pairs)]
        for copy in copies:
            copy.start()
    edge = jnp.zeros((width, 3 * channels), jnp.bfloat16)
    taps[0:width, :] = edge
    taps[width + cells : 2 * width + cells, :] = edge
    same_group = (
        bucket((channels, channels), 0, channels // GROUPS)
        == bucket((channels, channels), 1, channels // GROUPS)
    ).astype(jnp.float32).astype(jnp.bfloat16)
    column = lax.broadcasted_iota(jnp.int32, (1, width, channels), 1)

    def conv(values, layer):
        framed = values.reshape(height, width, channels)
        left = jnp.where(column == 0, 0.0, pltpu.roll(framed, 1, 1)).reshape(cells, channels)
        right = jnp.where(column == width - 1, 0.0, pltpu.roll(framed, width - 1, 1)).reshape(cells, channels)
        taps[width : width + cells, 0:channels] = left.astype(jnp.bfloat16)
        taps[width : width + cells, channels : 2 * channels] = values.astype(jnp.bfloat16)
        taps[width : width + cells, 2 * channels : 3 * channels] = right.astype(jnp.bfloat16)
        if stream:
            for row in range(3):
                copies[3 * layer + row].wait()
        lhs = jnp.concatenate([taps[row * width : row * width + cells, :] for row in range(3)], axis=1)
        return jnp.dot(lhs, kernels[layer].reshape(9 * channels, channels), preferred_element_type=jnp.float32)

    if picks:
        entering = entering_ref[...].astype(jnp.float32)
        start = jnp.where(lax.axis_index("section") == 0, entering, unpack(passed_ref, channels))
    else:
        start = passed_ref[...].astype(jnp.float32)
    middle = conv(silu(group_norm(start, same_group)), 0).astype(jnp.bfloat16).astype(jnp.float32)
    after = conv(silu(group_norm(middle, same_group)), 1)
    pack(out_ref, start + after)
    if stream:
        copies[-1].wait()


def spatial_part(height, width, devices, passed, weights, plan=None, entering=None, turn=0, later=None):
    cells, channels = height * width, weights.shape[-1]
    chunks = (devices,) + chunk_shape(cells // devices, channels)
    weights = weights.reshape(2, 3, 3 * channels, weights.shape[-1])
    stream = plan is None
    specs = [
        pl.BlockSpec(passed.shape, lambda i, *_: (0,) * passed.ndim),
        pl.BlockSpec(memory_space=pltpu.HBM if stream else pltpu.VMEM),
    ]
    operands = [passed, weights]
    if plan is not None:
        specs = [pl.BlockSpec((None, cells, channels), lambda i, order: (order[turn], 0, 0))] + specs
        operands = [plan, entering] + operands
    out_shape = jax.ShapeDtypeStruct(chunks, jnp.bfloat16)
    out_specs = pl.BlockSpec(chunks, lambda i, *_: (0, 0, 0))
    if stream:
        specs.append(pl.BlockSpec(memory_space=pltpu.HBM))
        operands.append(later)
        out_shape = [out_shape, jax.ShapeDtypeStruct(later.shape, later.dtype)]
        out_specs = [out_specs, pl.BlockSpec(memory_space=pltpu.VMEM)]
    return pl.pallas_call(
        functools.partial(spatial_kernel, height, width, plan is not None, stream),
        out_shape=out_shape,
        grid_spec=pltpu.PrefetchScalarGridSpec(
            num_scalar_prefetch=0 if plan is None else 1,
            grid=(1,),
            in_specs=specs,
            out_specs=out_specs,
            scratch_shapes=[pltpu.VMEM((cells + 2 * width, 3 * channels), jnp.bfloat16)]
            + ([pltpu.VMEM(weights.shape, jnp.bfloat16), pltpu.SemaphoreType.DMA((7,))] if stream else []),
        ),
        compiler_params=pltpu.CompilerParams(vmem_limit_bytes=(52 if stream else 24) * MIB),
    )(*operands)


def temporal_kernel(frames, items, in_ref, kernels, packed, outward, out_ref, taps):
    rows, channels = frames * items, outward.shape[-1]
    aligned = items % 16 == 0

    def conv(values, layer):
        if aligned:
            whole = values.astype(jnp.bfloat16)
            edge = jnp.zeros((items, channels), jnp.bfloat16)
            taps[0:items, 0:channels] = edge
            taps[items:rows, 0:channels] = whole[0 : rows - items]
            taps[:, channels : 2 * channels] = whole
            taps[0 : rows - items, 2 * channels : 3 * channels] = whole[items:rows]
            taps[rows - items : rows, 2 * channels : 3 * channels] = edge
        else:
            row = lax.broadcasted_iota(jnp.int32, (rows, channels), 0)
            before = jnp.where(row < items, 0.0, pltpu.roll(values, items, 0))
            behind = jnp.where(row >= rows - items, 0.0, pltpu.roll(values, rows - items, 0))
            taps[:, 0:channels] = before.astype(jnp.bfloat16)
            taps[:, channels : 2 * channels] = values.astype(jnp.bfloat16)
            taps[:, 2 * channels : 3 * channels] = behind.astype(jnp.bfloat16)
        return jnp.dot(taps[...], kernels[layer], preferred_element_type=jnp.float32)

    ones = jnp.ones((channels, LANES), jnp.bfloat16)
    start = unpack(in_ref, channels)
    middle = conv(silu(layer_norm(start.astype(jnp.bfloat16), ones)), 0).astype(jnp.bfloat16)
    after = (start + conv(silu(layer_norm(middle, ones)), 1)).astype(jnp.bfloat16)

    normed = layer_norm(after, ones).astype(jnp.bfloat16)
    taps[...] = jnp.dot(normed, packed[...], preferred_element_type=jnp.float32).astype(jnp.bfloat16)
    queries = taps[:, 0:channels]
    keys = taps[:, channels : 2 * channels]
    values = taps[:, 2 * channels : 3 * channels]

    head_size = channels // HEADS
    block = 16 if aligned else items
    size = frames * block
    apart = within((size, size), 0, block) != within((size, size), 1, block)
    blocked = jnp.where(apart, -1e30, 0.0)
    scale = head_size ** (-0.5) * LOG2_E
    groups = [(first, min(first + LANES, channels)) for first in range(0, channels, LANES)]
    tall = jnp.ones((size, LANES), jnp.bfloat16)

    def part(whole, first):
        if block == items:
            return whole
        return jnp.concatenate(
            [whole[f * items + first : f * items + first + block] for f in range(frames)], axis=0
        )

    mixed_blocks = []
    for first in range(0, items, block):
        q, k, v = part(queries, first), part(keys, first), part(values, first)
        mixed = []
        for low, high in groups:
            heads = (high - low) // head_size
            owner = bucket((size, high - low), 1, head_size)
            chosen = q[:, low:high]
            if heads > 1:
                chosen = jnp.concatenate(
                    [jnp.where(owner == head, chosen, jnp.zeros_like(chosen)) for head in range(heads)], axis=0
                )
            scores = lax.dot_general(
                k[:, low:high], chosen, (((1,), (1,)), ((), ())), preferred_element_type=jnp.float32
            )
            scores = scores * scale + jnp.concatenate([blocked] * heads, axis=1)
            top = jnp.max(scores, axis=0, keepdims=True)
            raised = jnp.exp2(scores - top).astype(jnp.bfloat16)
            both = lax.dot_general(raised, jnp.concatenate([tall, v[:, low:high]], axis=1), (((0,), (0,)), ((), ())), preferred_element_type=jnp.float32)
            share = both[:, LANES:] / both[:, : high - low]
            out = share[0:size]
            for head in range(1, heads):
                out = jnp.where(owner == head, share[head * size : (head + 1) * size], out)
            mixed.append(out.astype(jnp.bfloat16))
        mixed_blocks.append(jnp.concatenate(mixed, axis=1))
    if len(mixed_blocks) == 1:
        mixed = mixed_blocks[0]
    else:
        mixed = jnp.concatenate(
            [piece[f * block : (f + 1) * block] for f in range(frames) for piece in mixed_blocks], axis=0
        )
    result = after.astype(jnp.float32) + jnp.dot(mixed, outward[...], preferred_element_type=jnp.float32)
    pack(out_ref, result)


def temporal_part(frames, items, values, kernels, packed, outward):
    rows, channels = frames * items, outward.shape[-1]
    kernels = kernels.reshape(2, 3 * channels, kernels.shape[-1])
    resident = pl.BlockSpec(memory_space=pltpu.VMEM)
    return pl.pallas_call(
        functools.partial(temporal_kernel, frames, items),
        out_shape=jax.ShapeDtypeStruct(values.shape, jnp.bfloat16),
        in_specs=[resident] * 4,
        out_specs=pl.BlockSpec(memory_space=pltpu.VMEM),
        scratch_shapes=[
            pltpu.VMEM((rows, 3 * channels), jnp.bfloat16),
        ],
        compiler_params=pltpu.CompilerParams(vmem_limit_bytes=24 * MIB),
    )(values, kernels, packed, outward)


def collect_kernel(tick, *refs):
    in_ref, *_, out_ref, rows, sem = refs
    rows[...] = unpack(in_ref, rows.shape[-1]).astype(jnp.bfloat16)
    copy = pltpu.make_async_copy(rows, out_ref.at[tick], sem)
    copy.start()
    copy.wait()


def collect(tick, values, shape, outputs=None):
    before = [] if outputs is None else [outputs]
    return pl.pallas_call(
        functools.partial(collect_kernel, tick),
        out_shape=jax.ShapeDtypeStruct(shape, values.dtype),
        in_specs=[pl.BlockSpec(memory_space=pltpu.VMEM)] + [pl.BlockSpec(memory_space=pl.ANY)] * len(before),
        out_specs=pl.BlockSpec(memory_space=pl.ANY),
        scratch_shapes=[pltpu.VMEM(shape[1:], values.dtype), pltpu.SemaphoreType.DMA],
        input_output_aliases={1: 0} if before else {},
        compiler_params=pltpu.CompilerParams(vmem_limit_bytes=4 * MIB),
        cost_estimate=pl.CostEstimate(flops=0, bytes_accessed=4 * values.size, transcendentals=0),
    )(values, *before)


def shards(incoming, plan, waiting, spatial_weight, temporal_weight, attn_in, attn_out):
    clips, _, height, width, channels = incoming.shape
    cells = height * width
    devices = lax.axis_size("seq")
    share = cells // devices
    sections = lax.axis_size("section")
    entering = incoming.reshape(clips, cells, channels)
    current = waiting.reshape(cells, channels)
    ring = [(i, (i + 1) % sections) for i in range(sections)]
    outputs = None
    for tick in range(TICKS):
        if tick == 0:
            after, temporal = spatial_part(height, width, devices, current, spatial_weight[0], later=temporal_weight[0])
        else:
            passed, outputs = lax.optimization_barrier((lax.ppermute(current, "section", ring), outputs))
            after = spatial_part(height, width, devices, passed, spatial_weight[0], plan, entering, tick - 1)
        gathered = lax.all_to_all(after, "seq", split_axis=0, concat_axis=0, tiled=True)
        done = temporal_part(devices, share, gathered, temporal, attn_in[0], attn_out[0])
        current = lax.all_to_all(done, "seq", split_axis=0, concat_axis=0, tiled=True)
        outputs = collect(tick, current, (TICKS, cells, channels), outputs)
    return outputs.reshape(TICKS, 1, 1, height, width, channels)


def solution(mesh):
    return jax.shard_map(
        shards,
        mesh=mesh,
        in_specs=(
            P(None, "seq", None, None, None),
            P(),
            P("section", "seq", None, None, None),
            P("section", None, None, None, None),
            P("section", None, None, None, None),
            P("section", None, None),
            P("section", None, None),
        ),
        out_specs=P(None, "section", "seq", None, None, None),
        check_vma=False,
    )
```

```python
import functools

import jax
import jax.numpy as jnp
from jax import lax
from jax.experimental import pallas as pl
from jax.experimental.pallas import tpu as pltpu
from jax.sharding import PartitionSpec as P

HEADS = 5
GROUPS = 32
TICKS = 3
EPSILON = 1e-05
MIB = 1 << 20
LANES = 128
LOG2_E = 1.4426950408889634


def silu(values):
    half = 0.5 * values
    return half + half * jnp.tanh(half)


def bucket(shape, dim, size):
    index = lax.broadcasted_iota(jnp.int32, shape, dim).astype(jnp.float32)
    return jnp.floor((index + 0.5) * (1.0 / size))


def within(shape, dim, size):
    index = lax.broadcasted_iota(jnp.int32, shape, dim).astype(jnp.float32)
    return index - size * jnp.floor((index + 0.5) * (1.0 / size))


def chunk_shape(share, channels):
    if share % 16 == 0 and channels % LANES * 2 == LANES:
        return (share * channels // LANES, LANES)
    return (share, channels)


def pack(out_ref, values):
    devices, height, width = out_ref.shape
    rows, channels = values.shape
    share = rows // devices
    if width == channels:
        out_ref[...] = values.astype(jnp.bfloat16).reshape(out_ref.shape)
        return
    columns = channels // LANES
    for device in range(devices):
        own = values[device * share : (device + 1) * share]
        for column in range(columns):
            piece = own[:, column * LANES : (column + 1) * LANES]
            out_ref[device, column * share : (column + 1) * share, :] = piece.astype(jnp.bfloat16)
        last = own[:, columns * LANES :]
        piece = jnp.concatenate([last[: share // 2], last[share // 2 :]], axis=1)
        out_ref[device, columns * share :, :] = piece.astype(jnp.bfloat16)


def unpack(in_ref, channels):
    devices, height, width = in_ref.shape
    if width == channels:
        return in_ref[...].astype(jnp.float32).reshape(devices * height, channels)
    share = height * width // channels
    columns = channels // LANES
    rows = []
    for device in range(devices):
        pieces = [
            in_ref[device, column * share : (column + 1) * share, :].astype(jnp.float32) for column in range(columns)
        ]
        last = in_ref[device, columns * share :, :].astype(jnp.float32)
        pieces.append(jnp.concatenate([last[:, : LANES // 2], last[:, LANES // 2 :]], axis=0))
        rows.append(jnp.concatenate(pieces, axis=1))
    return jnp.concatenate(rows, axis=0)


def group_total(partial, same_group):
    high = partial.astype(jnp.bfloat16).astype(jnp.float32)
    rest = partial - high
    middle = rest.astype(jnp.bfloat16).astype(jnp.float32)
    low = rest - middle
    rows = jnp.concatenate([high, middle, low, jnp.zeros_like(low)], axis=0).astype(jnp.bfloat16)
    sums = jnp.dot(rows, same_group, preferred_element_type=jnp.float32)
    return jnp.sum(sums, axis=0, keepdims=True)


def group_norm(values, same_group):
    cells, channels = values.shape
    scale = 1.0 / (cells * (channels // GROUPS))
    partial = jnp.sum(values.reshape(-1, 8, channels), axis=0)
    center = group_total(partial, same_group) * scale
    own = jnp.sum(partial, axis=0, keepdims=True) * (1.0 / cells)
    squares = jnp.sum(jnp.square(values - own).reshape(-1, 8, channels), axis=0)
    squares = squares + jnp.square(own - center) * (cells / 8)
    spread = group_total(squares, same_group) * scale
    return (values - center) * lax.rsqrt(spread + EPSILON)


def layer_norm(values, ones):
    channels = values.shape[-1]

    def across(sums):
        pieces = -(-channels // sums.shape[-1])
        return jnp.concatenate([sums] * pieces, axis=-1)[:, :channels]

    floats = values.astype(jnp.float32)
    center = jnp.dot(values, ones, preferred_element_type=jnp.float32) * (1.0 / channels)
    shifted = floats - across(center)
    squares = jnp.square(shifted).astype(jnp.bfloat16)
    spread = jnp.dot(squares, ones, preferred_element_type=jnp.float32) * (1.0 / channels)
    return shifted * across(lax.rsqrt(spread + EPSILON))


def spatial_kernel(height, width, picks, stream, *refs):
    if picks:
        _, entering_ref, *refs = refs
    if stream:
        passed_ref, weight_ref, later_ref, out_ref, held_ref, taps, kernels, sems = refs
    else:
        passed_ref, weight_ref, out_ref, taps = refs
        kernels = weight_ref
    cells, channels = height * width, weight_ref.shape[-1]
    copies = []
    if stream:
        pairs = [(weight_ref.at[layer, row], kernels.at[layer, row]) for layer in range(2) for row in range(3)]
        pairs.append((later_ref, held_ref))
        copies = [pltpu.make_async_copy(source, target, sems.at[i]) for i, (source, target) in enumerate(pairs)]
        for copy in copies:
            copy.start()
    edge = jnp.zeros((width, 3 * channels), jnp.bfloat16)
    taps[0:width, :] = edge
    taps[width + cells : 2 * width + cells, :] = edge
    same_group = (
        bucket((channels, channels), 0, channels // GROUPS)
        == bucket((channels, channels), 1, channels // GROUPS)
    ).astype(jnp.float32).astype(jnp.bfloat16)
    column = lax.broadcasted_iota(jnp.int32, (1, width, channels), 1)

    def conv(values, layer):
        framed = values.reshape(height, width, channels)
        left = jnp.where(column == 0, 0.0, pltpu.roll(framed, 1, 1)).reshape(cells, channels)
        right = jnp.where(column == width - 1, 0.0, pltpu.roll(framed, width - 1, 1)).reshape(cells, channels)
        taps[width : width + cells, 0:channels] = left.astype(jnp.bfloat16)
        taps[width : width + cells, channels : 2 * channels] = values.astype(jnp.bfloat16)
        taps[width : width + cells, 2 * channels : 3 * channels] = right.astype(jnp.bfloat16)
        if stream:
            for row in range(3):
                copies[3 * layer + row].wait()
        lhs = jnp.concatenate([taps[row * width : row * width + cells, :] for row in range(3)], axis=1)
        return jnp.dot(lhs, kernels[layer].reshape(9 * channels, channels), preferred_element_type=jnp.float32)

    if picks:
        entering = entering_ref[...].astype(jnp.float32)
        start = jnp.where(lax.axis_index("section") == 0, entering, unpack(passed_ref, channels))
    else:
        start = passed_ref[...].astype(jnp.float32)
    middle = conv(silu(group_norm(start, same_group)), 0).astype(jnp.bfloat16).astype(jnp.float32)
    after = conv(silu(group_norm(middle, same_group)), 1)
    pack(out_ref, start + after)
    if stream:
        copies[-1].wait()


def spatial_part(height, width, devices, passed, weights, plan=None, entering=None, turn=0, later=None):
    cells, channels = height * width, weights.shape[-1]
    chunks = (devices,) + chunk_shape(cells // devices, channels)
    weights = weights.reshape(2, 3, 3 * channels, weights.shape[-1])
    stream = plan is None
    specs = [
        pl.BlockSpec(passed.shape, lambda i, *_: (0,) * passed.ndim),
        pl.BlockSpec(memory_space=pltpu.HBM if stream else pltpu.VMEM),
    ]
    operands = [passed, weights]
    if plan is not None:
        specs = [pl.BlockSpec((None, cells, channels), lambda i, order: (order[turn], 0, 0))] + specs
        operands = [plan, entering] + operands
    out_shape = jax.ShapeDtypeStruct(chunks, jnp.bfloat16)
    out_specs = pl.BlockSpec(chunks, lambda i, *_: (0, 0, 0))
    if stream:
        specs.append(pl.BlockSpec(memory_space=pltpu.HBM))
        operands.append(later)
        out_shape = [out_shape, jax.ShapeDtypeStruct(later.shape, later.dtype)]
        out_specs = [out_specs, pl.BlockSpec(memory_space=pltpu.VMEM)]
    return pl.pallas_call(
        functools.partial(spatial_kernel, height, width, plan is not None, stream),
        out_shape=out_shape,
        grid_spec=pltpu.PrefetchScalarGridSpec(
            num_scalar_prefetch=0 if plan is None else 1,
            grid=(1,),
            in_specs=specs,
            out_specs=out_specs,
            scratch_shapes=[pltpu.VMEM((cells + 2 * width, 3 * channels), jnp.bfloat16)]
            + ([pltpu.VMEM(weights.shape, jnp.bfloat16), pltpu.SemaphoreType.DMA((7,))] if stream else []),
        ),
        compiler_params=pltpu.CompilerParams(vmem_limit_bytes=(52 if stream else 24) * MIB),
    )(*operands)


def temporal_kernel(frames, items, in_ref, kernels, packed, outward, out_ref, taps):
    rows, channels = frames * items, outward.shape[-1]
    aligned = items % 16 == 0

    def conv(values, layer):
        if aligned:
            whole = values.astype(jnp.bfloat16)
            edge = jnp.zeros((items, channels), jnp.bfloat16)
            before = jnp.concatenate([edge, whole[0 : rows - items]], axis=0)
            behind = jnp.concatenate([whole[items:rows], edge], axis=0)
            lhs = jnp.concatenate([before, whole, behind], axis=1)
            return jnp.dot(lhs, kernels[layer], preferred_element_type=jnp.float32)
        else:
            row = lax.broadcasted_iota(jnp.int32, (rows, channels), 0)
            before = jnp.where(row < items, 0.0, pltpu.roll(values, items, 0))
            behind = jnp.where(row >= rows - items, 0.0, pltpu.roll(values, rows - items, 0))
            taps[:, 0:channels] = before.astype(jnp.bfloat16)
            taps[:, channels : 2 * channels] = values.astype(jnp.bfloat16)
            taps[:, 2 * channels : 3 * channels] = behind.astype(jnp.bfloat16)
        return jnp.dot(taps[...], kernels[layer], preferred_element_type=jnp.float32)

    ones = jnp.ones((channels, LANES), jnp.bfloat16)
    start = unpack(in_ref, channels)
    middle = conv(silu(layer_norm(start.astype(jnp.bfloat16), ones)), 0).astype(jnp.bfloat16)
    after = (start + conv(silu(layer_norm(middle, ones)), 1)).astype(jnp.bfloat16)

    normed = layer_norm(after, ones).astype(jnp.bfloat16)
    projected = jnp.dot(normed, packed[...], preferred_element_type=jnp.float32).astype(jnp.bfloat16)
    queries, keys, values = [projected[:, i * channels : (i + 1) * channels] for i in range(3)]

    head_size = channels // HEADS
    block = 16 if aligned else items
    size = frames * block
    apart = within((size, size), 0, block) != within((size, size), 1, block)
    blocked = jnp.where(apart, -1e30, 0.0)
    scale = head_size ** (-0.5) * LOG2_E
    groups = [(first, min(first + LANES, channels)) for first in range(0, channels, LANES)]
    tall = jnp.ones((size, LANES), jnp.bfloat16)

    def part(whole, first):
        if block == items:
            return whole
        return jnp.concatenate(
            [whole[f * items + first : f * items + first + block] for f in range(frames)], axis=0
        )

    mixed_blocks = []
    for first in range(0, items, block):
        q, k, v = part(queries, first), part(keys, first), part(values, first)
        mixed = []
        for low, high in groups:
            heads = (high - low) // head_size
            owner = bucket((size, high - low), 1, head_size)
            chosen = q[:, low:high]
            if heads > 1:
                chosen = jnp.concatenate(
                    [jnp.where(owner == head, chosen, jnp.zeros_like(chosen)) for head in range(heads)], axis=0
                )
            scores = lax.dot_general(
                k[:, low:high], chosen, (((1,), (1,)), ((), ())), preferred_element_type=jnp.float32
            )
            scores = scores * scale + jnp.concatenate([blocked] * heads, axis=1)
            top = jnp.max(scores, axis=0, keepdims=True)
            raised = jnp.exp2(scores - top).astype(jnp.bfloat16)
            both = lax.dot_general(raised, jnp.concatenate([tall, v[:, low:high]], axis=1), (((0,), (0,)), ((), ())), preferred_element_type=jnp.float32)
            share = both[:, LANES:] / both[:, : high - low]
            out = share[0:size]
            for head in range(1, heads):
                out = jnp.where(owner == head, share[head * size : (head + 1) * size], out)
            mixed.append(out.astype(jnp.bfloat16))
        mixed_blocks.append(jnp.concatenate(mixed, axis=1))
    if len(mixed_blocks) == 1:
        mixed = mixed_blocks[0]
    else:
        mixed = jnp.concatenate(
            [piece[f * block : (f + 1) * block] for f in range(frames) for piece in mixed_blocks], axis=0
        )
    result = after.astype(jnp.float32) + jnp.dot(mixed, outward[...], preferred_element_type=jnp.float32)
    pack(out_ref, result)


def temporal_part(frames, items, values, kernels, packed, outward):
    rows, channels = frames * items, outward.shape[-1]
    kernels = kernels.reshape(2, 3 * channels, kernels.shape[-1])
    resident = pl.BlockSpec(memory_space=pltpu.VMEM)
    return pl.pallas_call(
        functools.partial(temporal_kernel, frames, items),
        out_shape=jax.ShapeDtypeStruct(values.shape, jnp.bfloat16),
        in_specs=[resident] * 4,
        out_specs=pl.BlockSpec(memory_space=pltpu.VMEM),
        scratch_shapes=[
            pltpu.VMEM((rows, 3 * channels), jnp.bfloat16),
        ],
        compiler_params=pltpu.CompilerParams(vmem_limit_bytes=24 * MIB),
    )(values, kernels, packed, outward)


def collect_kernel(tick, *refs):
    in_ref, *_, out_ref, rows, sem = refs
    rows[...] = unpack(in_ref, rows.shape[-1]).astype(jnp.bfloat16)
    copy = pltpu.make_async_copy(rows, out_ref.at[tick], sem)
    copy.start()
    copy.wait()


def collect(tick, values, shape, outputs=None):
    before = [] if outputs is None else [outputs]
    return pl.pallas_call(
        functools.partial(collect_kernel, tick),
        out_shape=jax.ShapeDtypeStruct(shape, values.dtype),
        in_specs=[pl.BlockSpec(memory_space=pltpu.VMEM)] + [pl.BlockSpec(memory_space=pl.ANY)] * len(before),
        out_specs=pl.BlockSpec(memory_space=pl.ANY),
        scratch_shapes=[pltpu.VMEM(shape[1:], values.dtype), pltpu.SemaphoreType.DMA],
        input_output_aliases={1: 0} if before else {},
        compiler_params=pltpu.CompilerParams(vmem_limit_bytes=4 * MIB),
        cost_estimate=pl.CostEstimate(flops=0, bytes_accessed=4 * values.size, transcendentals=0),
    )(values, *before)


def shards(incoming, plan, waiting, spatial_weight, temporal_weight, attn_in, attn_out):
    clips, _, height, width, channels = incoming.shape
    cells = height * width
    devices = lax.axis_size("seq")
    share = cells // devices
    sections = lax.axis_size("section")
    entering = incoming.reshape(clips, cells, channels)
    current = waiting.reshape(cells, channels)
    ring = [(i, (i + 1) % sections) for i in range(sections)]
    outputs = None
    for tick in range(TICKS):
        if tick == 0:
            after, temporal = spatial_part(height, width, devices, current, spatial_weight[0], later=temporal_weight[0])
        else:
            passed, outputs = lax.optimization_barrier((lax.ppermute(current, "section", ring), outputs))
            after = spatial_part(height, width, devices, passed, spatial_weight[0], plan, entering, tick - 1)
        gathered = lax.all_to_all(after, "seq", split_axis=0, concat_axis=0, tiled=True)
        done = temporal_part(devices, share, gathered, temporal, attn_in[0], attn_out[0])
        current = lax.all_to_all(done, "seq", split_axis=0, concat_axis=0, tiled=True)
        outputs = collect(tick, current, (TICKS, cells, channels), outputs)
    return outputs.reshape(TICKS, 1, 1, height, width, channels)


def solution(mesh):
    return jax.shard_map(
        shards,
        mesh=mesh,
        in_specs=(
            P(None, "seq", None, None, None),
            P(),
            P("section", "seq", None, None, None),
            P("section", None, None, None, None),
            P("section", None, None, None, None),
            P("section", None, None),
            P("section", None, None),
        ),
        out_specs=P(None, "section", "seq", None, None, None),
        check_vma=False,
    )
```
